32 devices in a mesh: groups: 2 (over x), seq: 8 (over z, y), exp: 2 (over core).
Axes of the slice: x: 2, y: 2, z: 4, core: 2. Of those that a mesh axis runs over, the one named last changes fastest.
Arguments:
- queries: bfloat16 [4096, 2048], P(('groups', 'seq'), 'exp'), parts along dimension 0, may hold values from -6 to 6
- key_rows: bfloat16 [4096, 256], P(('groups', 'seq'), 'exp'), parts along dimension 0, may hold values from -6 to 6
- values: bfloat16 [4096, 256], P(('groups', 'seq'), 'exp'), parts along dimension 0, may hold values from -6 to 6
- sink_logit: float32 [32], P('exp'), may hold values from 0 to 5
- o_weight: bfloat16 [2048, 1440], P('exp'), may hold values from -0.5 to 0.5
- residual: bfloat16 [4096, 1440], P(('groups', 'seq')), parts along dimension 0, may hold values from -30 to 30
- norm_gain: float32 [1440], replicated, may hold values from 0.1 to 1.9
- routes: int32 [4096, 4], P(('groups', 'seq')), parts along dimension 0, may hold values from 0 to 7, all different within a row; in each aligned block of 128 rows (0 to 127, 128 to 255, ...) at most 128 rows name the same one
- gate_codes: int32 [4096, 4], P(('groups', 'seq')), parts along dimension 0, may hold values from 1 to 256
- w_gate: bfloat16 [8, 1440, 1440], P('seq', None, 'exp'), may hold values from -0.15625 to 0.15625
- w_up: bfloat16 [8, 1440, 1440], P('seq', None, 'exp'), may hold values from -0.15625 to 0.15625
- w_down: bfloat16 [8, 1440, 1440], P('seq', 'exp'), may hold values from -0.15625 to 0.15625
Outputs:
- attended: bfloat16 [4096, 1440], P(('groups', 'seq', 'exp')), parts along dimension 0
- expert_mix: bfloat16 [4096, 1440], P(('groups', 'seq', 'exp')), parts along dimension 0
The draws below stay inside these ranges and needn't reach their ends.
There are 2 independent parts, one for each index of `groups`. The reference program is written for one: setup_inputs(seed, part) draws one part's arguments, and reference() takes and returns one part's arrays. A program takes and returns all parts, laid end to end along the dimension named above; an argument that names none is the same for every part. Nothing has to cross between parts.
Inputs may be any that keep to these rules, and one draw needn't show every extreme that they name: `routes`: each row names 4 different experts; in each aligned block of 128 rows no expert is named by more than 128 rows, and in some block one expert is named by exactly 128 rows.
All inputs are finite; a program needn't handle non-finite values.
Results may differ from the reference program's by a relative error of at most 0.013.
Values may be sent and summed in bfloat16 or wider, within the bound.
No kernel may reach another device: no remote copies, remote signals or barrier semaphores. Data moves between devices by JAX's collectives and lax.ppermute only.
A program may use at most 128 MiB of HBM per device.

```python
import math
import jax
import jax.numpy as jnp
import numpy as np
from jax import lax

D = 1440
HEADS = 32
KV_HEADS = 4
HEAD_DIM = 64
WINDOW = 128
FF = 1440
TOP = 4
TOK_DEV = 256
TOKENS = 2048
EXPERTS = 8
ROWS_DEV = 128
CAP = 128


def pair_draw(key):
    query_key = jax.random.fold_in(key, 101)
    kv_key = jax.random.fold_in(key, 102)
    query_vals = jnp.clip(jax.random.normal(query_key, (TOKENS, HEADS * HEAD_DIM), jnp.float32), -4.0, 4.0)
    key_vals = jnp.clip(jax.random.normal(kv_key, (TOKENS, KV_HEADS * HEAD_DIM), jnp.float32), -4.0, 4.0)
    return (query_vals, key_vals)


def draw_queries(key, part):
    return pair_draw(key)[0].astype(jnp.bfloat16)


def draw_key_rows(key, part):
    return pair_draw(key)[1].astype(jnp.bfloat16)


def draw_residual(key, part):
    base_key = jax.random.fold_in(key, 201)
    row_key = jax.random.fold_in(key, 202)
    col_key = jax.random.fold_in(key, 203)
    base = jax.random.normal(base_key, (TOKENS, D), jnp.float32)
    row_scale = jnp.exp(jax.random.uniform(row_key, (TOKENS, 1), jnp.float32, jnp.log(0.3), jnp.log(3.0)))
    col_scale = jnp.exp(jax.random.uniform(col_key, (1, D), jnp.float32, jnp.log(0.3), jnp.log(3.0)))
    return jnp.clip(base * row_scale * col_scale, -30.0, 30.0).astype(jnp.bfloat16)


def touch_ends(values, rng, smallest, high):
    index_at = [jax.random.randint(jax.random.fold_in(rng, axis), (), 0, length) for axis, length in enumerate(values.shape)]
    widest = values.shape.index(max(values.shape))
    beside = index_at[:widest] + [(index_at[widest] + 1) % values.shape[widest]] + index_at[widest + 1:]
    return values.at[tuple(index_at)].set(smallest).at[tuple(beside)].set(high)


def block_scale(stream_key, extent, split, smallest, high):
    def one(axis_at, parts):
        draws = jax.random.uniform(jax.random.fold_in(jax.random.fold_in(stream_key, 6), axis_at), (parts,), jnp.float32, smallest / len(split), high / len(split))
        return jnp.repeat(jnp.exp(draws), extent[axis_at] // parts).reshape((-1,) + (1,) * (len(extent) - axis_at - 1))

    factor_of = one(*split[0])
    for cut in split[1:]:
        factor_of = factor_of * one(*cut)
    return factor_of


def shared_out(stream_key, own, number, rows, number_of, top, reach, slope):
    order = jax.random.permutation(stream_key, number_of)
    packed, ordinary = load_shares(number_of, rows * top, reach, slope, True), load_shares(number_of, rows * top, reach, slope, False)
    places = jnp.arange(number_of)

    def named(sizes, turn):
        used = int((sizes > 0).sum())
        fixed = max(1, used // 4)
        passed = fixed + (places - fixed + turn * (used - fixed)) % max(1, number_of - fixed)
        return jnp.zeros((number_of,), jnp.int32).at[order[jnp.where(places < fixed, places, passed)]].set(jnp.asarray(sizes, jnp.int32))

    sizes = jnp.where(number % 4 == 0, named(packed, number // 4), named(ordinary, number - number // 4 - 1))
    mixed = jax.random.permutation(jax.random.fold_in(own, 3), number_of)
    donor, taker = mixed[0:number_of // 2 * 2:2], mixed[1:number_of // 2 * 2:2]
    margin = jnp.minimum(sizes[donor] - 1, reach - sizes[taker]) // 2
    margin = jnp.where((donor == order[0]) | (taker == order[0]) | (sizes[taker] == 0), 0, jnp.maximum(margin, 0))
    passed = jax.random.randint(jax.random.fold_in(own, 4), (number_of // 2,), 0, 1 << 20) % (margin + 1)
    sizes = sizes.at[donor].add(-passed).at[taker].add(passed)
    labels = jnp.searchsorted(jnp.cumsum(sizes), jnp.arange(rows * top), side="right").astype(jnp.int32)
    table = labels.reshape(top, rows).T
    table = table[jax.random.permutation(jax.random.fold_in(own, 1), rows)]
    turn = jax.random.randint(jax.random.fold_in(own, 2), (rows, 1), 0, top)
    return jnp.take_along_axis(table, (jnp.arange(top)[None, :] + turn) % top, axis=1)


def load_shares(amount, total, bound, skew, full):
    weights = [(1 << 20) // math.isqrt(rank ** skew) + 1 for rank in range(1, amount + 1)]
    largest = bound if full else min(bound, max(-(-total // amount), total * weights[0] // sum(weights)))
    least = 1 if total - largest >= amount - 1 else 0
    holding, rest = [largest] + [least] * (amount - 1), total - largest - least * (amount - 1)
    while rest > 0:
        candidates = [i for i in range(1, amount) if holding[i] < largest] or [i for i in range(1, amount) if holding[i] < bound]
        pool, remaining = sum([weights[i] for i in candidates]), rest
        for i in candidates:
            extra = min(bound - holding[i], max(1, remaining * weights[i] // pool), rest)
            holding[i] = holding[i] + extra
            rest = rest - extra
    return np.array(holding)


def scatter_about(key, dims, scale, reach, shards=(), held_as=jnp.bfloat16):
    gain = block_scale(key, dims, shards, -0.22, 0.18) if shards else 1.0
    values = jax.random.normal(key, dims, jnp.float32) * scale * gain
    return jnp.minimum(jnp.maximum(values, -reach), reach).astype(held_as)


def setup_inputs(seed: int = 0, part: int = 0) -> dict:
    arg_keys = jax.random.split(jax.random.key(seed), 13)
    part_splits = jax.random.split(jax.random.fold_in(arg_keys[12], part), 13)
    queries = draw_queries(jax.random.fold_in(jax.random.fold_in(arg_keys[12], part), 71), part)
    key_rows = draw_key_rows(jax.random.fold_in(jax.random.fold_in(arg_keys[12], part), 71), part)
    values = scatter_about(part_splits[2], (TOKENS, KV_HEADS * HEAD_DIM), 1.0, 6.0, ((0, 8), (1, 2)))
    sink_logit = jnp.clip(5.0 * jax.random.uniform(arg_keys[3], (HEADS,), jnp.float32) ** block_scale(arg_keys[3], (HEADS,), ((0, 2),), -0.2, 0.2), 0.0, 5.0)
    o_weight = scatter_about(arg_keys[4], (HEADS * HEAD_DIM, D), (HEADS * HEAD_DIM // 16) ** -0.5, 0.5, ((0, 2),))
    residual = draw_residual(jax.random.fold_in(jax.random.fold_in(arg_keys[12], part), 71), part)
    norm_gain = jnp.clip(1.0 + 0.18 * jax.random.normal(arg_keys[6], (D,), jnp.float32), 0.1, 1.9)
    routes_keys = jax.random.split(jax.random.fold_in(part_splits[7], 1), TOKENS // ROWS_DEV)
    routes_turns = jax.random.permutation(jax.random.fold_in(part_splits[7], 3), TOKENS // ROWS_DEV)
    routes = jax.vmap(lambda own, number: shared_out(jax.random.fold_in(part_splits[7], 2), own, number, ROWS_DEV, EXPERTS, TOP, CAP, 2))(routes_keys, routes_turns).reshape((TOKENS, TOP))
    gate_codes = touch_ends(jax.random.randint(part_splits[8], (TOKENS, TOP), 1, 257), jax.random.fold_in(part_splits[8], 1), 1, 256).astype(jnp.int32)
    w_gate = scatter_about(arg_keys[9], (EXPERTS, D, FF), D ** -0.5, 0.15625, ((0, 8), (2, 2)))
    w_up = scatter_about(arg_keys[10], (EXPERTS, D, FF), D ** -0.5, 0.15625, ((0, 8), (2, 2)))
    w_down = scatter_about(arg_keys[11], (EXPERTS, FF, D), FF ** -0.5, 0.15625, ((0, 8), (1, 2)))
    return {"queries": queries, "key_rows": key_rows, "values": values, "sink_logit": sink_logit, "o_weight": o_weight, "residual": residual, "norm_gain": norm_gain, "routes": routes, "gate_codes": gate_codes, "w_gate": w_gate, "w_up": w_up, "w_down": w_down}


def swiglu(gate_val, up_val):
    return (up_val + 1.0) * gate_val * jax.nn.sigmoid(1.702 * gate_val)

def rms_norm(stream, norm_gain):
    widened = stream.astype(jnp.float32)
    spread = lax.optimization_barrier(jnp.mean(widened * widened, axis=-1, keepdims=True))
    return (widened * lax.rsqrt(spread + 1e-05) * norm_gain).astype(jnp.bfloat16)

def window_attention(queries, key_rows, values, sink_logit):
    group_size = HEADS // KV_HEADS
    blocks = TOKENS // TOK_DEV
    kv_width = KV_HEADS * HEAD_DIM
    padded_keys = jnp.concatenate([jnp.zeros((WINDOW, kv_width), key_rows.dtype), key_rows], axis=0)
    padded_values = jnp.concatenate([jnp.zeros((WINDOW, kv_width), values.dtype), values], axis=0)
    sink_vals = sink_logit.astype(jnp.float32).reshape(KV_HEADS, group_size)[:, :, None, None]

    def one_block(block_start):
        block_q = lax.dynamic_slice_in_dim(queries, block_start, TOK_DEV, 0).astype(jnp.float32)
        block_q = block_q.reshape(TOK_DEV, KV_HEADS, group_size, HEAD_DIM)
        block_k = lax.dynamic_slice_in_dim(padded_keys, block_start, TOK_DEV + WINDOW, 0).astype(jnp.float32)
        block_k = block_k.reshape(TOK_DEV + WINDOW, KV_HEADS, HEAD_DIM)
        block_v = lax.dynamic_slice_in_dim(padded_values, block_start, TOK_DEV + WINDOW, 0).astype(jnp.float32)
        block_v = block_v.reshape(TOK_DEV + WINDOW, KV_HEADS, HEAD_DIM)
        scores = jnp.einsum('tgjd,ugd->gjtu', block_q, block_k, precision=lax.Precision.HIGHEST) * HEAD_DIM ** (-0.5)
        query_pos = block_start + jnp.arange(TOK_DEV, dtype=jnp.int32)[:, None]
        key_pos = block_start - WINDOW + jnp.arange(TOK_DEV + WINDOW, dtype=jnp.int32)[None, :]
        allowed = (key_pos <= query_pos) & (key_pos > query_pos - WINDOW) & (key_pos >= 0)
        scores = jnp.where(allowed, scores, -1e+30)
        ceiling = jnp.maximum(lax.optimization_barrier(jnp.max(scores, axis=-1, keepdims=True)), sink_vals)
        raised = jnp.exp(scores - ceiling)
        denominator = lax.optimization_barrier(jnp.sum(raised, axis=-1, keepdims=True)) + jnp.exp(sink_vals - ceiling)
        weights = (raised / denominator).astype(jnp.bfloat16)
        mixed = jnp.einsum('gjtu,ugd->tgjd', weights.astype(jnp.float32), block_v, precision=lax.Precision.HIGHEST)
        return mixed.astype(jnp.bfloat16).reshape(TOK_DEV, HEADS * HEAD_DIM)
    starts = jnp.arange(blocks, dtype=jnp.int32) * TOK_DEV
    return lax.map(one_block, starts).reshape(TOKENS, HEADS * HEAD_DIM)

def mix_experts(normed, routes, gate_codes, w_gate, w_up, w_down):
    sources = TOKENS // ROWS_DEV
    block_ids = routes.reshape(sources, ROWS_DEV * TOP)
    matches = (block_ids[:, :, None] == jnp.arange(EXPERTS, dtype=jnp.int32)[None, None, :]).astype(jnp.int32)
    within = lax.optimization_barrier(jnp.sum((jnp.cumsum(matches, axis=1) - 1) * matches, axis=2))
    column = (jnp.arange(sources, dtype=jnp.int32)[:, None] * CAP + within).reshape(-1)
    pair_ids = block_ids.reshape(-1)
    token_of = jnp.arange(TOKENS * TOP, dtype=jnp.int32) // TOP
    inbox_rows = jnp.zeros((EXPERTS, sources * CAP, D), jnp.bfloat16).at[pair_ids, column].set(normed[token_of])

    def one_expert(operands):
        rows_in, gate_w, up_w, down_w = operands
        gate_val = jnp.dot(rows_in, gate_w, preferred_element_type=jnp.float32)
        up_val = jnp.dot(rows_in, up_w, preferred_element_type=jnp.float32)
        hidden = swiglu(gate_val, up_val).astype(jnp.bfloat16)
        return jnp.dot(hidden, down_w, preferred_element_type=jnp.float32)
    outputs = lax.map(one_expert, (inbox_rows, w_gate, w_up, w_down))
    picked = outputs[pair_ids, column]
    code_vals = gate_codes.astype(jnp.float32)
    shares = code_vals / lax.optimization_barrier(jnp.sum(code_vals, axis=1, keepdims=True))
    mixture = lax.optimization_barrier(jnp.sum(picked.reshape(TOKENS, TOP, D) * shares[:, :, None], axis=1))
    return mixture.astype(jnp.bfloat16)

def reference(queries, key_rows, values, sink_logit, o_weight, residual, norm_gain, routes, gate_codes, w_gate, w_up, w_down):
    heads_out = window_attention(queries, key_rows, values, sink_logit)
    attn_proj = jnp.dot(heads_out, o_weight, preferred_element_type=jnp.float32)
    attended = (residual.astype(jnp.float32) + attn_proj).astype(jnp.bfloat16)
    normed = rms_norm(attended, norm_gain)
    return (attended, mix_experts(normed, routes, gate_codes, w_gate, w_up, w_down))
```

```python
import functools

import jax
import jax.numpy as jnp
from jax import lax
from jax.experimental import pallas as pl
from jax.experimental.pallas import tpu as pltpu
from jax.sharding import PartitionSpec as P

HEAD_DIM = 64
WINDOW = 128
TOP = 4
BF16_ROWS = 16
F32 = jnp.float32
BF16 = jnp.bfloat16
VMEM = pl.BlockSpec(memory_space=pltpu.VMEM)
SMEM = pl.BlockSpec(memory_space=pltpu.SMEM)


def swiglu(gate_val, up_val):
    return (up_val + 1.0) * gate_val * jax.nn.sigmoid(1.702 * gate_val)


def heads_of(q_rows, past, present, sink_ref, earlier, first):
    kv_width = past.shape[1] // 2
    kv_heads = kv_width // HEAD_DIM
    group = q_rows.shape[1] // kv_width
    q_cols = (q_rows * HEAD_DIM ** (-0.5)).T
    both = jnp.concatenate([past, present], axis=0)
    outs = []
    for g in range(kv_heads):
        keys = both[:, g * HEAD_DIM : (g + 1) * HEAD_DIM]
        vals = both[:, kv_width + g * HEAD_DIM : kv_width + (g + 1) * HEAD_DIM].T
        for j in range(0, group, 2):
            pair = [g * group + j, g * group + j + 1]
            q_pair = jnp.concatenate([q_cols[h * HEAD_DIM : (h + 1) * HEAD_DIM] for h in pair], axis=1)
            scores = jnp.dot(keys, q_pair, preferred_element_type=F32)
            seen = jnp.where(earlier, jnp.where(first, -1e30, scores[:WINDOW]), scores[WINDOW:])
            sink = jnp.concatenate([jnp.full((1, WINDOW), sink_ref[h], F32) for h in pair], axis=1)
            ceiling = jnp.maximum(jnp.max(seen, axis=0, keepdims=True), sink)
            raised = jnp.exp(seen - ceiling)
            total = jnp.sum(raised, axis=0, keepdims=True) + jnp.exp(sink - ceiling)
            spread = jnp.concatenate([jnp.where(earlier, raised, 0.0), jnp.where(earlier, 0.0, raised)], axis=0)
            mixed = jnp.dot(vals, spread.astype(BF16), preferred_element_type=F32) / total
            mixed = mixed.astype(BF16)
            outs += [mixed[:, :WINDOW], mixed[:, WINDOW:]]
    return jnp.concatenate(outs, axis=0)


def front_kernel(
    code_rows, place, sink_a, sink_b, q_a, q_b, kv_a, kv_b, rim_a, rim_b, ow_a, ow_b,
    resid, gain, routes, codes, attended_ref, parcel_ref,
):
    core, first = place[0], place[1] == 1
    start = pl.multiple_of(core * WINDOW, WINDOW)
    rows = pl.ds(start, WINDOW)
    shape = (WINDOW, 2 * WINDOW)
    key_at = lax.broadcasted_iota(jnp.int32, shape, 0)
    query_at = lax.rem(lax.broadcasted_iota(jnp.int32, shape, 1), WINDOW)
    earlier = key_at > query_at
    lead = core == 0
    projected = None
    for q, kv, rim, sink, ow in ((q_a, kv_a, rim_a, sink_a, ow_a), (q_b, kv_b, rim_b, sink_b, ow_b)):
        past = jnp.where(lead, rim[...], kv[:WINDOW, :])
        heads = heads_of(q[rows, :], past, kv[rows, :], sink, earlier, first)
        term = jnp.dot(ow[...], heads, preferred_element_type=F32)
        projected = term if projected is None else projected + term
    attended = (resid[:, rows].astype(F32) + projected).astype(BF16)
    attended_ref[...] = attended
    widened = attended.astype(F32)
    spread = jnp.mean(widened * widened, axis=0, keepdims=True)
    gains = jnp.broadcast_to(gain[...], (WINDOW, gain.shape[1])).T
    parcel_ref[code_rows:, :] = (widened * lax.rsqrt(spread + 1e-05) * gains).astype(BF16)
    if code_rows:
        expert = lax.broadcasted_iota(jnp.int32, (code_rows, WINDOW), 0)
        table = jnp.zeros((code_rows, WINDOW), F32)
        for k in range(TOP):
            named = jnp.broadcast_to(routes[k : k + 1, rows], expert.shape) == expert
            table += jnp.where(named, jnp.broadcast_to(codes[k : k + 1, rows], expert.shape).astype(F32), 0.0)
        parcel_ref[:code_rows, :] = table.astype(BF16)


def front(code_rows, queries, key_rows, values, sink_logit, o_weight, residual, norm_gain, routes, gate_codes):
    seq, core = lax.axis_index("seq"), lax.axis_index("exp")
    count, cores = lax.axis_size("seq"), lax.axis_size("exp")
    place = jnp.stack([core, jnp.where((seq == 0) & (core == 0), 1, 0)]).astype(jnp.int32)
    kv = jnp.concatenate([key_rows, values], axis=1)
    rim = kv[kv.shape[0] - WINDOW :]

    def to_next(source_core):
        steps = [(s * cores + source_core, (s + 1) * cores) for s in range(count - 1)]
        return lax.ppermute(rim, ("seq", "exp"), steps)

    rim_a, rim_b = to_next(0), to_next(1)
    ow = o_weight.T
    kv_b, q_b, sink_b, ow_b = [swapped(value) for value in (kv, queries, sink_logit, ow)]
    features = residual.shape[1]
    block = residual.shape[0] // cores
    return pl.pallas_call(
        functools.partial(front_kernel, code_rows),
        out_shape=(
            jax.ShapeDtypeStruct((features, block), BF16),
            jax.ShapeDtypeStruct((code_rows + features, block), BF16),
        ),
        in_specs=[SMEM] * 3 + [VMEM] * 12,
        out_specs=(VMEM, VMEM),
        cost_estimate=pl.CostEstimate(flops=2 * 10**9, bytes_accessed=10**7, transcendentals=10**6),
        compiler_params=pltpu.CompilerParams(vmem_limit_bytes=40 * 2**20),
        name="front",
    )(
        place, sink_logit, sink_b, queries, q_b, kv, kv_b, rim_a, rim_b, ow, ow_b,
        residual.T, norm_gain[None, :], routes.T, gate_codes.T,
    )


def swapped(value):
    return lax.ppermute(value, "exp", [(0, 1), (1, 0)])


def expert_kernel(code_rows, count, place, *refs):
    parcels, weights, outs = refs[:count], refs[count : count + 6], refs[count + 6 :]
    rows = jnp.concatenate([ref[code_rows:, :] for ref in parcels], axis=1).T
    total = None
    for w_gate, w_up, w_down in (weights[:3], weights[3:]):
        gate_val = jnp.dot(rows, w_gate[...], preferred_element_type=F32)
        up_val = jnp.dot(rows, w_up[...], preferred_element_type=F32)
        hidden = swiglu(gate_val, up_val).astype(BF16)
        term = jnp.dot(hidden, w_down[...], preferred_element_type=F32)
        total = term if total is None else total + term
    total = total.T
    for i in range(count):
        codes = parcels[i][:code_rows, :].astype(F32)
        mine = lax.broadcasted_iota(jnp.int32, codes.shape, 0) == place[0]
        code = jnp.sum(jnp.where(mine, codes, 0.0), axis=0, keepdims=True)
        share = code / jnp.sum(codes, axis=0, keepdims=True)
        outs[i][...] = (total[:, i * WINDOW : (i + 1) * WINDOW] * share).astype(BF16)


def expert_terms(code_rows, expert, parcels, weights):
    count = len(parcels)
    features = parcels[0].shape[0] - code_rows
    flops = 2 * count * WINDOW * features * 3 * 2 * weights[0].shape[1]
    return pl.pallas_call(
        functools.partial(expert_kernel, code_rows, count),
        out_shape=[jax.ShapeDtypeStruct((features, WINDOW), BF16)] * count,
        in_specs=[SMEM] + [VMEM] * (count + 6),
        out_specs=[VMEM] * count,
        cost_estimate=pl.CostEstimate(flops=flops, bytes_accessed=14 * 10**6, transcendentals=10**5),
        compiler_params=pltpu.CompilerParams(vmem_limit_bytes=48 * 2**20),
        name="experts",
    )(expert, *parcels, *weights)


def ring_of(count):
    order = list(range(0, count, 2)) + list(range(count - 1, 0, -2))
    right = [(order[i], order[(i + 1) % count]) for i in range(count)]
    return right, [(target, source) for source, target in right]


def mixed_by_ring(parcel, code_rows, weights):
    count = lax.axis_size("seq")
    right, left = ring_of(count)
    far = count // 2
    expert = lax.axis_index("seq").astype(jnp.int32)[None]
    to_right = functools.partial(lax.ppermute, axis_name="seq", perm=right)
    to_left = functools.partial(lax.ppermute, axis_name="seq", perm=left)
    apply = functools.partial(expert_terms, code_rows, expert, weights=weights)
    features = parcel.shape[0] - code_rows
    half = features // 2
    cut = code_rows + half
    from_left, from_right = parcel, parcel
    terms = {}
    for k in range(1, far):
        from_left, from_right = to_right(from_left), to_left(from_right)
        terms[-k], terms[k] = apply([from_left, from_right])
        if k == 1:
            terms[0] = apply([parcel])[0]
    upper, lower = to_right(from_left[:cut]), to_left(from_right[cut:])
    farthest = apply([jnp.concatenate([upper, lower], axis=0)])[0]
    add = lambda a, b: (a.astype(F32) + b.astype(F32)).astype(BF16)
    going_right, going_left = to_right(farthest[:half]), to_left(farthest[half:])
    for k in range(far - 1, 0, -1):
        if k == far - 1:
            going_right = jnp.concatenate([add(terms[k][:half], going_right), terms[k][half:]], axis=0)
            going_left = jnp.concatenate([terms[-k][:half], add(terms[-k][half:], going_left)], axis=0)
        else:
            going_right, going_left = add(terms[k], going_right), add(terms[-k], going_left)
        going_right, going_left = to_right(going_right), to_left(going_left)
    return (terms[0].astype(F32) + going_right.astype(F32) + going_left.astype(F32)).astype(BF16)


def pack_rows(normed, expert_ids, gate_codes, expert_count, capacity):
    pair_ids = expert_ids.reshape(-1)
    matches = (pair_ids[:, None] == jnp.arange(expert_count, dtype=jnp.int32)[None, :]).astype(
        jnp.int32
    )
    within = jnp.sum((jnp.cumsum(matches, axis=0) - 1) * matches, axis=1)
    sources = normed[jnp.arange(pair_ids.shape[0], dtype=jnp.int32) // expert_ids.shape[1]]
    outbox = jnp.zeros((expert_count * capacity, normed.shape[1]), normed.dtype)
    outbox = outbox.at[pair_ids * capacity + within].set(sources)
    code_vals = gate_codes.astype(F32)
    shares = (code_vals / jnp.sum(code_vals, axis=1, keepdims=True)).reshape(-1)
    return (outbox, pair_ids, within, shares)


def mixed_by_packing(normed, routes, gate_codes, weights, expert_count, capacity):
    w_gate, w_up, w_down = weights
    owners, block = lax.axis_size("exp"), normed.shape[0]
    owner_pos = lax.axis_index("exp")
    own = lambda value: lax.dynamic_slice_in_dim(value, owner_pos * block, block, 0)
    outbox, pair_ids, within, shares = pack_rows(
        normed, own(routes), own(gate_codes), expert_count, capacity
    )
    outbox = outbox.reshape(expert_count, capacity, normed.shape[1])
    exchange = functools.partial(lax.all_to_all, axis_name="seq", split_axis=0, concat_axis=0, tiled=True)
    arrived = lax.all_gather(exchange(outbox), "exp", axis=0, tiled=True)
    flat_rows = arrived.reshape(-1, arrived.shape[-1])
    gate_val = jnp.dot(flat_rows, w_gate, preferred_element_type=F32)
    up_val = jnp.dot(flat_rows, w_up, preferred_element_type=F32)
    hidden = swiglu(gate_val, up_val).astype(BF16)
    partial_value = jnp.dot(hidden, w_down, preferred_element_type=F32).reshape(arrived.shape)
    whole = lax.psum_scatter(partial_value.astype(BF16), "exp", scatter_dimension=0, tiled=True)
    picked = exchange(whole)[pair_ids, within].astype(F32)
    mixture = jnp.sum((picked * shares[:, None]).reshape(-1, TOP, normed.shape[1]), axis=1)
    return mixture.astype(BF16)


def local(
    queries,
    key_rows,
    values,
    sink_logit,
    o_weight,
    residual,
    norm_gain,
    routes,
    gate_codes,
    w_gate,
    w_up,
    w_down,
):
    block_rows = residual.shape[0] // lax.axis_size("exp")
    expert_count = w_gate.shape[0] * lax.axis_size("seq")
    capacity = max(2, 2 * block_rows * TOP // expert_count)
    weights = (w_gate[0], w_up[0], w_down[0])
    attention = (queries, key_rows, values, sink_logit, o_weight, residual, norm_gain, routes, gate_codes)
    if capacity < block_rows:
        attended, normed = front(0, *attention)
        mixture = mixed_by_packing(normed.T, routes, gate_codes, weights, expert_count, capacity)
        return (attended.T, mixture)
    code_rows = -(-expert_count // BF16_ROWS) * BF16_ROWS
    attended, parcel = front(code_rows, *attention)
    weights = weights + tuple(swapped(weight) for weight in weights)
    return (attended.T, mixed_by_ring(parcel, code_rows, weights).T)


def solution(mesh):
    placed = (
        P(("groups", "seq"), "exp"),
        P(("groups", "seq"), "exp"),
        P(("groups", "seq"), "exp"),
        P("exp"),
        P("exp", None),
        P(("groups", "seq"), None),
        P(),
        P(("groups", "seq"), None),
        P(("groups", "seq"), None),
        P("seq", None, "exp"),
        P("seq", None, "exp"),
        P("seq", "exp", None),
    )
    return jax.shard_map(
        local,
        mesh=mesh,
        in_specs=placed,
        out_specs=(P(("groups", "seq", "exp"), None), P(("groups", "seq", "exp"), None)),
        check_vma=False,
    )
```

```python
import functools

import jax
import jax.numpy as jnp
from jax import lax
from jax.experimental import pallas as pl
from jax.experimental.pallas import tpu as pltpu
from jax.sharding import PartitionSpec as P

HEAD_DIM = 64
WINDOW = 128
TOP = 4
BF16_ROWS = 16
F32 = jnp.float32
BF16 = jnp.bfloat16
VMEM = pl.BlockSpec(memory_space=pltpu.VMEM)
SMEM = pl.BlockSpec(memory_space=pltpu.SMEM)
ANY = pl.BlockSpec(memory_space=pl.ANY)
in_hbm = functools.partial(pltpu.with_memory_space_constraint, memory_space=pltpu.HBM)
in_vmem = functools.partial(pltpu.with_memory_space_constraint, memory_space=pltpu.VMEM)


def swiglu(gate_val, up_val):
    return (up_val + 1.0) * gate_val * jax.nn.sigmoid(1.702 * gate_val)


def heads_of(q_cols, past, present, sinks, first):
    kv_width = past.shape[1] // 2
    group = q_cols.shape[0] // kv_width
    shape = (WINDOW, group * WINDOW)
    query_at = lax.rem(lax.broadcasted_iota(jnp.int32, shape, 1), WINDOW)
    earlier = lax.broadcasted_iota(jnp.int32, shape, 0) > query_at
    both = jnp.concatenate([past, present], axis=0)
    outs = []
    for g in range(kv_width // HEAD_DIM):
        keys = both[:, g * HEAD_DIM : (g + 1) * HEAD_DIM]
        vals = both[:, kv_width + g * HEAD_DIM : kv_width + (g + 1) * HEAD_DIM].T
        heads = range(g * group, (g + 1) * group)
        q_group = jnp.concatenate([q_cols[h * HEAD_DIM : (h + 1) * HEAD_DIM] for h in heads], axis=1)
        scores = jnp.dot(keys, q_group, preferred_element_type=F32)
        seen = jnp.where(earlier, jnp.where(first, -1e30, scores[:WINDOW]), scores[WINDOW:])
        sink = jnp.concatenate([jnp.broadcast_to(sinks[:, h : h + 1], (1, WINDOW)) for h in heads], axis=1)
        ceiling = jnp.maximum(jnp.max(seen, axis=0, keepdims=True), sink)
        raised = jnp.exp(seen - ceiling)
        total = jnp.sum(raised, axis=0, keepdims=True) + jnp.exp(sink - ceiling)
        spread = jnp.concatenate([jnp.where(earlier, raised, 0.0), jnp.where(earlier, 0.0, raised)], axis=0)
        mixed = jnp.dot(vals, spread.astype(BF16), preferred_element_type=F32) * (1.0 / total)
        mixed = mixed.astype(BF16)
        outs += [mixed[:, i * WINDOW : (i + 1) * WINDOW] for i in range(group)]
    return jnp.concatenate(outs, axis=0)


def pack_kernel(place, sink, k, v, q, packed, rim, sems):
    count, last, width = k.shape[0], k.shape[0] - WINDOW, k.shape[1]
    base = 2 * count + BF16_ROWS
    rows = pl.ds(pl.multiple_of((1 - place[0]) * WINDOW, WINDOW), WINDOW)
    moves = [
        (k.at[last:, :], rim.at[:WINDOW, :]),
        (v.at[last:, :], rim.at[WINDOW:, :]),
        (k, packed.at[:count, :]),
        (v, packed.at[count : 2 * count, :]),
    ]
    for j in range(q.shape[1] // width):
        to = base + j * WINDOW
        moves.append((q.at[rows, j * width : (j + 1) * width], packed.at[to : to + WINDOW, :]))
    copies = [pltpu.make_async_copy(source, target, sems.at[i]) for i, (source, target) in enumerate(moves)]
    for copy in copies:
        copy.start()
    shape = (BF16_ROWS, width)
    lane, row = (lax.broadcasted_iota(jnp.int32, shape, i) for i in (1, 0))
    left = jnp.zeros(shape, F32)
    for h in range(sink.shape[0]):
        left = jnp.where(lane == h, sink[h], left)
    terms = jnp.zeros(shape, F32)
    for i in range(3):
        term = left.astype(BF16).astype(F32)
        terms = jnp.where(row == i, term, terms)
        left = left - term
    packed[2 * count : base, :] = terms.astype(BF16)
    for copy in copies:
        copy.wait()


def pack(place, sink_logit, key_rows, values, queries):
    rows, width = key_rows.shape
    blocks = queries.shape[1] // width
    return pl.pallas_call(
        pack_kernel,
        out_shape=[
            jax.ShapeDtypeStruct((n, width), BF16) for n in (2 * rows + BF16_ROWS + blocks * WINDOW, 2 * WINDOW)
        ],
        in_specs=[SMEM, SMEM, ANY, ANY, ANY],
        out_specs=[VMEM, VMEM],
        scratch_shapes=[pltpu.SemaphoreType.DMA((4 + blocks,))],
        cost_estimate=pl.CostEstimate(flops=0, bytes_accessed=4 * key_rows.size, transcendentals=0),
        compiler_params=pltpu.CompilerParams(vmem_limit_bytes=4 * 2**20),
        name="pack",
    )(place, sink_logit, in_hbm(key_rows), in_hbm(values), in_hbm(queries))


def front_kernel(code_rows, place, packed_a, rim_a, packed_b, *refs):
    hbm, outs, scratch = refs[:6], refs[6 : 9 if code_rows else 7], refs[9 if code_rows else 7 :]
    q_a, ow_a, ow_b, resid, routes, codes = hbm
    core, first = place[0], place[1] == 1
    start = pl.multiple_of(core * WINDOW, WINDOW)
    rows = pl.ds(start, WINDOW)
    held, sems = scratch[:-1], scratch[-1]
    sources = (q_a.at[rows, :], ow_a, ow_b, resid.at[:, rows], routes.at[:, rows], codes.at[:, rows])
    copies = [pltpu.make_async_copy(source, held[i], sems.at[i]) for i, source in enumerate(sources)]
    for copy in copies:
        copy.start()
    lead = core == 0
    width = rim_a.shape[1]
    blocks = held[0].shape[1] // width
    base = packed_a.shape[0] - blocks * WINDOW
    count = (base - BF16_ROWS) // 2
    tail = packed_b.at[packed_a.shape[0] :, :]
    later = pl.ds(pl.multiple_of(count + start, WINDOW), WINDOW)

    def attend(packed, rim, q_blocks):
        past = jnp.concatenate(
            [
                jnp.where(lead, rim[:WINDOW, :], packed[:WINDOW, :]),
                jnp.where(lead, rim[WINDOW:, :], packed[count : count + WINDOW, :]),
            ],
            axis=1,
        )
        present = jnp.concatenate([packed[rows, :], packed[later, :]], axis=1)
        terms = packed[2 * count : base, :].astype(F32)
        sinks = terms[0:1] + terms[1:2] + terms[2:3]
        q_cols = jnp.concatenate([(block * HEAD_DIM ** (-0.5)).T for block in q_blocks], axis=0)
        return heads_of(q_cols, past, present, sinks, first)

    theirs = attend(
        packed_b, tail, [packed_b[base + j * WINDOW : base + (j + 1) * WINDOW, :] for j in range(blocks)]
    )
    copies[0].wait()
    ours = attend(packed_a, rim_a, [held[0][:, j * width : (j + 1) * width] for j in range(blocks)])
    copies[2].wait()
    projected = jnp.dot(held[2][...], theirs, preferred_element_type=F32)
    copies[1].wait()
    projected += jnp.dot(held[1][...], ours, preferred_element_type=F32)
    for copy in copies[3:]:
        copy.wait()
    attended = (held[3][...].astype(F32) + projected).astype(BF16)
    outs[0][...] = attended
    if code_rows:
        expert = lax.broadcasted_iota(jnp.int32, (code_rows, WINDOW), 0)
        table = jnp.zeros((code_rows, WINDOW), F32)
        for k in range(TOP):
            named = jnp.broadcast_to(held[4][k : k + 1, :], expert.shape) == expert
            table += jnp.where(named, jnp.broadcast_to(held[5][k : k + 1, :], expert.shape).astype(F32), 0.0)
        outs[1][:code_rows, :] = table.astype(BF16)
        half = half_of(attended.shape[0])
        outs[1][code_rows:, :] = attended[:half]
        outs[2][...] = attended[half:]


def front(code_rows, queries, key_rows, values, sink_logit, o_weight, residual, routes, gate_codes):
    seq, core = lax.axis_index("seq"), lax.axis_index("exp")
    place = jnp.stack([core, jnp.where((seq == 0) & (core == 0), 1, 0)]).astype(jnp.int32)
    ow_b = swapped(o_weight.T)
    packed, rim = pack(place, sink_logit, key_rows, values, queries)
    rim_a = lax.ppermute(rim, "seq", [(s, s + 1) for s in range(lax.axis_size("seq") - 1)])
    packed_b = swapped(jnp.concatenate([packed, rim_a], axis=0))
    features, block = residual.shape[1], residual.shape[0] // lax.axis_size("exp")
    half = half_of(features)
    shapes = [(features, block)] + ([(code_rows + half, block), (features - half, block)] if code_rows else [])
    held = [queries[:WINDOW], o_weight.T, o_weight.T]
    held += [residual.T[:, :WINDOW], routes.T[:, :WINDOW], gate_codes.T[:, :WINDOW]]
    outs = pl.pallas_call(
        functools.partial(front_kernel, code_rows),
        out_shape=[jax.ShapeDtypeStruct(shape, BF16) for shape in shapes],
        in_specs=[SMEM] + [VMEM] * 3 + [ANY] * 6,
        out_specs=[VMEM] * len(shapes),
        scratch_shapes=[pltpu.VMEM(h.shape, h.dtype) for h in held] + [pltpu.SemaphoreType.DMA((len(held),))],
        cost_estimate=pl.CostEstimate(flops=2 * 10**9, bytes_accessed=10**7, transcendentals=10**6),
        compiler_params=pltpu.CompilerParams(vmem_limit_bytes=20 * 2**20),
        name="front",
    )(
        place, packed, rim_a, packed_b, in_hbm(queries), in_hbm(o_weight.T), in_hbm(ow_b),
        in_hbm(residual.T), in_hbm(routes.T), in_hbm(gate_codes.T),
    )
    return outs, packed_b[:BF16_ROWS]


def swapped(value):
    return lax.ppermute(value, "exp", [(0, 1), (1, 0)])


def after(value, *earlier):
    return lax.optimization_barrier((value, *earlier))[0]


def rms_norm(stream, norm_gain):
    widened = stream.astype(F32)
    spread = jnp.mean(widened * widened, axis=-1, keepdims=True)
    return (widened * lax.rsqrt(spread + 1e-05) * norm_gain).astype(BF16)


def expert_kernel(code_rows, place, gain, upper, lower, *refs):
    weights, (out_upper, out_lower) = refs[:6], refs[6:]
    rows = rms_norm(jnp.concatenate([upper[code_rows:, :], lower[...]], axis=0).T, gain[...])
    total = None
    for w_gate, w_up, w_down in (weights[:3], weights[3:]):
        gate_val = jnp.dot(rows, w_gate[...], preferred_element_type=F32)
        up_val = jnp.dot(rows, w_up[...], preferred_element_type=F32)
        hidden = swiglu(gate_val, up_val).astype(BF16)
        term = jnp.dot(hidden, w_down[...], preferred_element_type=F32)
        total = term if total is None else total + term
    codes = upper[:code_rows, :].astype(F32)
    mine = lax.broadcasted_iota(jnp.int32, codes.shape, 0) == place[0]
    code = jnp.sum(jnp.where(mine, codes, 0.0), axis=0, keepdims=True)
    term = (total.T * (code / jnp.sum(codes, axis=0, keepdims=True))).astype(BF16)
    half = out_upper.shape[0]
    out_upper[...] = term[:half]
    out_lower[...] = term[half:]


def expert_terms(code_rows, expert, gain, weights, parcel):
    features = gain.shape[1]
    half = half_of(features)
    flops = 2 * WINDOW * features * 3 * 2 * weights[0].shape[1]
    return pl.pallas_call(
        functools.partial(expert_kernel, code_rows),
        out_shape=[jax.ShapeDtypeStruct((n, WINDOW), BF16) for n in (half, features - half)],
        in_specs=[SMEM] + [VMEM] * 9,
        out_specs=[VMEM] * 2,
        cost_estimate=pl.CostEstimate(flops=flops, bytes_accessed=10**6, transcendentals=10**5),
        compiler_params=pltpu.CompilerParams(vmem_limit_bytes=24 * 2**20),
        name="experts",
    )(expert, gain, *parcel, *weights)


def half_of(features):
    return features // 2 // BF16_ROWS * BF16_ROWS


def ring_of(count):
    order = list(range(0, count, 2)) + list(range(count - 1, 0, -2))
    right = [(order[i], order[(i + 1) % count]) for i in range(count)]
    return right, [(target, source) for source, target in right]


def add(a, b):
    return (a.astype(F32) + b.astype(F32)).astype(BF16)


def mixed_by_ring(parcel, code_rows, gain, weights):
    count = lax.axis_size("seq")
    right, left = ring_of(count)
    far = count // 2
    expert = lax.axis_index("seq").astype(jnp.int32)[None]
    to_right = functools.partial(lax.ppermute, axis_name="seq", perm=right)
    to_left = functools.partial(lax.ppermute, axis_name="seq", perm=left)
    apply = functools.partial(expert_terms, code_rows, expert, gain, weights)
    at = {0: parcel}
    at[-1], at[1] = [to_right(half) for half in parcel], [to_left(half) for half in parcel]
    terms, waited = {}, ()
    for k in range(2, far + 1):
        upper_left = to_right(after(at[1 - k][0], *waited))
        upper_right = to_left(after(at[k - 1][0], *waited)) if k < far else None
        if k > 2:
            terms[k - 2] = apply(after(at[k - 2], *at[1 - k][:1], *at[k - 1][:1]))
            waited = terms[k - 2]
        lower_left = to_right(after(at[1 - k][1], *waited)) if k < far else None
        lower_right = to_left(after(at[k - 1][1], *waited))
        terms[1 - k] = apply(after(at[1 - k], *waited))
        waited = terms[1 - k]
        at[-k], at[k] = [upper_left, lower_left], [upper_right, lower_right]
    opposite = [at[-far][0], at[far][1]]
    left_up = to_left(terms[1 - far][0])
    terms[far - 1] = apply(after(at[far - 1], *waited))
    right_low = to_right(terms[far - 1][1])
    farthest = apply(after(opposite, *terms[far - 1]))
    right_up, left_low = to_right(farthest[0]), to_left(farthest[1])
    terms[0] = apply(after(parcel, left_up, right_low))
    for k in range(far - 1, 0, -1):
        if k > 1:
            going = add(terms[1 - k][0], left_up), add(terms[k - 1][1], right_low)
            left_up, right_low = to_left(going[0]), to_right(going[1])
        going = add(terms[-k][1], left_low), add(terms[k][0], right_up)
        if k == far - 1:
            going = after(going, *terms[0])
        left_low, right_up = to_left(going[0]), to_right(going[1])
    near, left_up, right_low = after((terms[0], left_up, right_low), left_low, right_up)
    upper = near[0].astype(F32) + left_up.astype(F32) + right_up.astype(F32)
    lower = near[1].astype(F32) + left_low.astype(F32) + right_low.astype(F32)
    return jnp.concatenate([upper, lower], axis=0).astype(BF16)


def pack_rows(normed, expert_ids, gate_codes, expert_count, capacity):
    pair_ids = expert_ids.reshape(-1)
    matches = (pair_ids[:, None] == jnp.arange(expert_count, dtype=jnp.int32)[None, :]).astype(
        jnp.int32
    )
    within = jnp.sum((jnp.cumsum(matches, axis=0) - 1) * matches, axis=1)
    sources = normed[jnp.arange(pair_ids.shape[0], dtype=jnp.int32) // expert_ids.shape[1]]
    outbox = jnp.zeros((expert_count * capacity, normed.shape[1]), normed.dtype)
    outbox = outbox.at[pair_ids * capacity + within].set(sources)
    code_vals = gate_codes.astype(F32)
    shares = (code_vals / jnp.sum(code_vals, axis=1, keepdims=True)).reshape(-1)
    return (outbox, pair_ids, within, shares)


def mixed_by_packing(normed, routes, gate_codes, weights, expert_count, capacity):
    w_gate, w_up, w_down = weights
    owners, block = lax.axis_size("exp"), normed.shape[0]
    owner_pos = lax.axis_index("exp")
    own = lambda value: lax.dynamic_slice_in_dim(value, owner_pos * block, block, 0)
    outbox, pair_ids, within, shares = pack_rows(
        normed, own(routes), own(gate_codes), expert_count, capacity
    )
    outbox = outbox.reshape(expert_count, capacity, normed.shape[1])
    exchange = functools.partial(lax.all_to_all, axis_name="seq", split_axis=0, concat_axis=0, tiled=True)
    arrived = lax.all_gather(exchange(outbox), "exp", axis=0, tiled=True)
    flat_rows = arrived.reshape(-1, arrived.shape[-1])
    gate_val = jnp.dot(flat_rows, w_gate, preferred_element_type=F32)
    up_val = jnp.dot(flat_rows, w_up, preferred_element_type=F32)
    hidden = swiglu(gate_val, up_val).astype(BF16)
    partial_value = jnp.dot(hidden, w_down, preferred_element_type=F32).reshape(arrived.shape)
    whole = lax.psum_scatter(partial_value.astype(BF16), "exp", scatter_dimension=0, tiled=True)
    picked = exchange(whole)[pair_ids, within].astype(F32)
    mixture = jnp.sum((picked * shares[:, None]).reshape(-1, TOP, normed.shape[1]), axis=1)
    return mixture.astype(BF16)


def local(
    queries,
    key_rows,
    values,
    sink_logit,
    o_weight,
    residual,
    norm_gain,
    routes,
    gate_codes,
    w_gate,
    w_up,
    w_down,
):
    block_rows = residual.shape[0] // lax.axis_size("exp")
    expert_count = w_gate.shape[0] * lax.axis_size("seq")
    capacity = max(2, 2 * block_rows * TOP // expert_count)
    weights = (w_gate[0], w_up[0], w_down[0])
    attention = (queries, key_rows, values, sink_logit, o_weight, residual, routes, gate_codes)
    if capacity < block_rows:
        (attended,), _ = front(0, *attention)
        attended = attended.T
        normed = rms_norm(attended, norm_gain)
        return (attended, mixed_by_packing(normed, routes, gate_codes, weights, expert_count, capacity))
    code_rows = -(-expert_count // BF16_ROWS) * BF16_ROWS
    (attended, *parcel), arrived = front(code_rows, *attention)
    gate_b, up_b = (swapped(after(weight, arrived)) for weight in weights[:2])
    down_b = swapped(after(weights[2], gate_b, up_b, attended))
    weights = [in_vmem(weight) for weight in (*weights, gate_b, up_b, down_b)]
    return (attended.T, mixed_by_ring(parcel, code_rows, norm_gain[None, :], weights).T)


def solution(mesh):
    placed = (
        P(("groups", "seq"), "exp"),
        P(("groups", "seq"), "exp"),
        P(("groups", "seq"), "exp"),
        P("exp"),
        P("exp", None),
        P(("groups", "seq"), None),
        P(),
        P(("groups", "seq"), None),
        P(("groups", "seq"), None),
        P("seq", None, "exp"),
        P("seq", None, "exp"),
        P("seq", "exp", None),
    )
    return jax.shard_map(
        local,
        mesh=mesh,
        in_specs=placed,
        out_specs=(P(("groups", "seq", "exp"), None), P(("groups", "seq", "exp"), None)),
        check_vma=False,
    )
```

```python
import functools

import jax
import jax.numpy as jnp
from jax import lax
from jax.experimental import pallas as pl
from jax.experimental.pallas import tpu as pltpu
from jax.sharding import PartitionSpec as P

HEAD_DIM = 64
WINDOW = 128
TOP = 4
BF16_ROWS = 16
F32 = jnp.float32
BF16 = jnp.bfloat16
VMEM = pl.BlockSpec(memory_space=pltpu.VMEM)
SMEM = pl.BlockSpec(memory_space=pltpu.SMEM)
ANY = pl.BlockSpec(memory_space=pl.ANY)
in_hbm = functools.partial(pltpu.with_memory_space_constraint, memory_space=pltpu.HBM)
in_vmem = functools.partial(pltpu.with_memory_space_constraint, memory_space=pltpu.VMEM)


def swiglu(gate_val, up_val):
    return (up_val + 1.0) * gate_val * jax.nn.sigmoid(1.702 * gate_val)


def heads_of(q_cols, past, present, sinks, first):
    kv_width = past.shape[1] // 2
    group = q_cols.shape[0] // kv_width
    shape = (WINDOW, group * WINDOW)
    query_at = lax.rem(lax.broadcasted_iota(jnp.int32, shape, 1), WINDOW)
    earlier = lax.broadcasted_iota(jnp.int32, shape, 0) > query_at
    both = jnp.concatenate([past, present], axis=0)
    outs = []
    for g in range(kv_width // HEAD_DIM):
        keys = both[:, g * HEAD_DIM : (g + 1) * HEAD_DIM]
        vals = both[:, kv_width + g * HEAD_DIM : kv_width + (g + 1) * HEAD_DIM].T
        heads = range(g * group, (g + 1) * group)
        q_group = jnp.concatenate([q_cols[h * HEAD_DIM : (h + 1) * HEAD_DIM] for h in heads], axis=1)
        scores = jnp.dot(keys, q_group, preferred_element_type=F32)
        seen = jnp.where(earlier, jnp.where(first, -1e30, scores[:WINDOW]), scores[WINDOW:])
        sink = jnp.concatenate([jnp.broadcast_to(sinks[:, h : h + 1], (1, WINDOW)) for h in heads], axis=1)
        ceiling = jnp.maximum(jnp.max(seen, axis=0, keepdims=True), sink)
        raised = jnp.exp(seen - ceiling)
        total = jnp.sum(raised, axis=0, keepdims=True) + jnp.exp(sink - ceiling)
        spread = jnp.concatenate([jnp.where(earlier, raised, 0.0), jnp.where(earlier, 0.0, raised)], axis=0)
        mixed = jnp.dot(vals, spread.astype(BF16), preferred_element_type=F32) * (1.0 / total)
        mixed = mixed.astype(BF16)
        outs += [mixed[:, i * WINDOW : (i + 1) * WINDOW] for i in range(group)]
    return jnp.concatenate(outs, axis=0)


def pack_kernel(place, sink, gain, k, v, q, packed, gains, sems):
    count, width = k.shape
    base = 2 * count + BF16_ROWS
    rows = pl.ds(pl.multiple_of((1 - place[0]) * WINDOW, WINDOW), WINDOW)
    moves = [
        (k, packed.at[:count, :]),
        (v, packed.at[count : 2 * count, :]),
    ]
    for j in range(q.shape[1] // width):
        to = base + j * WINDOW
        moves.append((q.at[rows, j * width : (j + 1) * width], packed.at[to : to + WINDOW, :]))
    copies = [pltpu.make_async_copy(source, target, sems.at[i]) for i, (source, target) in enumerate(moves)]
    for copy in copies:
        copy.start()
    shape = (BF16_ROWS, width)
    lane, row = (lax.broadcasted_iota(jnp.int32, shape, i) for i in (1, 0))
    left = jnp.zeros(shape, F32)
    for h in range(sink.shape[0]):
        left = jnp.where(lane == h, sink[h], left)
    terms = jnp.zeros(shape, F32)
    for i in range(3):
        term = left.astype(BF16).astype(F32)
        terms = jnp.where(row == i, term, terms)
        left = left - term
    packed[2 * count : base, :] = terms.astype(BF16)
    gains[...] = jnp.broadcast_to(gain[...], (WINDOW, gain.shape[1])).T
    for copy in copies:
        copy.wait()


def rim_kernel(k, v, rim, sems):
    last = k.shape[0] - WINDOW
    copies = [
        pltpu.make_async_copy(k.at[last:, :], rim.at[:WINDOW, :], sems.at[0]),
        pltpu.make_async_copy(v.at[last:, :], rim.at[WINDOW:, :], sems.at[1]),
    ]
    for copy in copies:
        copy.start()
    for copy in copies:
        copy.wait()


def pack_rim(key_rows, values):
    return pl.pallas_call(
        rim_kernel,
        out_shape=jax.ShapeDtypeStruct((2 * WINDOW, key_rows.shape[1]), BF16),
        in_specs=[ANY, ANY],
        out_specs=VMEM,
        scratch_shapes=[pltpu.SemaphoreType.DMA((2,))],
        cost_estimate=pl.CostEstimate(flops=0, bytes_accessed=4 * key_rows.size, transcendentals=0),
        compiler_params=pltpu.CompilerParams(vmem_limit_bytes=4 * 2**20),
        name="rim",
    )(in_hbm(key_rows), in_hbm(values))


def pack(place, sink_logit, norm_gain, key_rows, values, queries):
    rows, width = key_rows.shape
    blocks = queries.shape[1] // width
    return pl.pallas_call(
        pack_kernel,
        out_shape=[
            jax.ShapeDtypeStruct((2 * rows + BF16_ROWS + blocks * WINDOW, width), BF16),
            jax.ShapeDtypeStruct((norm_gain.shape[0], WINDOW), F32),
        ],
        in_specs=[SMEM, SMEM, VMEM, ANY, ANY, ANY],
        out_specs=[VMEM, VMEM],
        scratch_shapes=[pltpu.SemaphoreType.DMA((2 + blocks,))],
        cost_estimate=pl.CostEstimate(flops=0, bytes_accessed=4 * key_rows.size, transcendentals=0),
        compiler_params=pltpu.CompilerParams(vmem_limit_bytes=4 * 2**20),
        name="pack",
    )(place, in_hbm(sink_logit), norm_gain[None, :], in_hbm(key_rows), in_hbm(values), in_hbm(queries))


def front_kernel(code_rows, place, gains, packed_a, rim_a, packed_b, rim_b, ow_b, *refs):
    hbm, outs, scratch = refs[:5], refs[5 : 8 if code_rows else 6], refs[8 if code_rows else 6 :]
    q_a, ow_a, resid, routes, codes = hbm
    core, first = place[0], place[1] == 1
    start = pl.multiple_of(core * WINDOW, WINDOW)
    rows = pl.ds(start, WINDOW)
    held, sems = scratch[:-1], scratch[-1]
    sources = (q_a.at[rows, :], ow_a, resid.at[:, rows], routes.at[:, rows], codes.at[:, rows])
    copies = [pltpu.make_async_copy(source, held[i], sems.at[i]) for i, source in enumerate(sources)]
    for copy in copies:
        copy.start()
    lead = core == 0
    width = rim_a.shape[1]
    blocks = held[0].shape[1] // width
    base = packed_a.shape[0] - blocks * WINDOW
    count = (base - BF16_ROWS) // 2
    later = pl.ds(pl.multiple_of(count + start, WINDOW), WINDOW)

    def attend(packed, rim, q_blocks):
        past = jnp.concatenate(
            [
                jnp.where(lead, rim[:WINDOW, :], packed[:WINDOW, :]),
                jnp.where(lead, rim[WINDOW:, :], packed[count : count + WINDOW, :]),
            ],
            axis=1,
        )
        present = jnp.concatenate([packed[rows, :], packed[later, :]], axis=1)
        terms = packed[2 * count : base, :].astype(F32)
        sinks = terms[0:1] + terms[1:2] + terms[2:3]
        q_cols = jnp.concatenate([(block * HEAD_DIM ** (-0.5)).T for block in q_blocks], axis=0)
        return heads_of(q_cols, past, present, sinks, first)

    theirs = attend(
        packed_b, rim_b, [packed_b[base + j * WINDOW : base + (j + 1) * WINDOW, :] for j in range(blocks)]
    )
    copies[0].wait()
    ours = attend(packed_a, rim_a, [held[0][:, j * width : (j + 1) * width] for j in range(blocks)])
    projected = jnp.dot(ow_b[...], theirs, preferred_element_type=F32)
    copies[1].wait()
    projected += jnp.dot(held[1][...], ours, preferred_element_type=F32)
    for copy in copies[2:]:
        copy.wait()
    attended = (held[2][...].astype(F32) + projected).astype(BF16)
    outs[0][...] = attended
    if code_rows:
        expert = lax.broadcasted_iota(jnp.int32, (code_rows, WINDOW), 0)
        table = jnp.zeros((code_rows, WINDOW), F32)
        for k in range(TOP):
            named = jnp.broadcast_to(held[3][k : k + 1, :], expert.shape) == expert
            table += jnp.where(named, jnp.broadcast_to(held[4][k : k + 1, :], expert.shape).astype(F32), 0.0)
        widened = attended.astype(F32)
        spread = jnp.mean(widened * widened, axis=0, keepdims=True)
        normed = (widened * lax.rsqrt(spread + 1e-05) * gains[...]).astype(BF16)
        body = normed.shape[0] // WINDOW * WINDOW
        blocks = [normed[j : j + WINDOW].T for j in range(0, body, WINDOW)]
        parcel = jnp.concatenate([table.astype(BF16), normed[body:], *blocks], axis=0)
        outs[1][...] = parcel[: outs[1].shape[0]]
        outs[2][...] = parcel[outs[1].shape[0] :]


def front(code_rows, queries, key_rows, values, sink_logit, o_weight, residual, norm_gain, routes, gate_codes, weights):
    seq, core = lax.axis_index("seq"), lax.axis_index("exp")
    place = jnp.stack([core, jnp.where((seq == 0) & (core == 0), 1, 0)]).astype(jnp.int32)
    ow_b = swapped(o_weight.T)
    steps = [(s, s + 1) for s in range(lax.axis_size("seq") - 1)]
    rim = pack_rim(key_rows, values)
    rim_a = lax.ppermute(rim, "seq", steps)
    packed, gains = pack(place, sink_logit, norm_gain, key_rows, values, queries)
    packed, rim_a = after(packed, rim_a)
    packed_b, rim_b = swapped(packed), swapped(rim_a)
    weights, rim_b = after(weights, rim_b)
    features, block = residual.shape[1], residual.shape[0] // lax.axis_size("exp")
    half = half_of(features)
    shapes = [(features, block)] + ([(code_rows + half, block), (features - half, block)] if code_rows else [])
    held = [queries[:WINDOW], o_weight.T]
    held += [residual.T[:, :WINDOW], routes.T[:, :WINDOW], gate_codes.T[:, :WINDOW]]
    outs = pl.pallas_call(
        functools.partial(front_kernel, code_rows),
        out_shape=[jax.ShapeDtypeStruct(shape, BF16) for shape in shapes],
        in_specs=[SMEM] + [VMEM] * 6 + [ANY] * 5,
        out_specs=[VMEM] * len(shapes),
        scratch_shapes=[pltpu.VMEM(h.shape, h.dtype) for h in held] + [pltpu.SemaphoreType.DMA((len(held),))],
        cost_estimate=pl.CostEstimate(flops=2 * 10**9, bytes_accessed=10**7, transcendentals=10**6),
        compiler_params=pltpu.CompilerParams(vmem_limit_bytes=20 * 2**20),
        name="front",
    )(
        place, gains, packed, rim_a, packed_b, rim_b, in_vmem(ow_b), in_hbm(queries), in_hbm(o_weight.T),
        in_hbm(residual.T), in_hbm(routes.T), in_hbm(gate_codes.T),
    )
    return outs, weights


def swapped(value):
    return lax.ppermute(value, "exp", [(0, 1), (1, 0)])


def after(value, earlier):
    return lax.optimization_barrier((value, earlier))


def rms_norm(stream, norm_gain):
    widened = stream.astype(F32)
    spread = jnp.mean(widened * widened, axis=-1, keepdims=True)
    return (widened * lax.rsqrt(spread + 1e-05) * norm_gain).astype(BF16)


def expert_kernel(code_rows, place, upper, lower, *refs):
    weights, (out_upper, out_lower) = refs[:6], refs[6:]
    parcel = jnp.concatenate([upper[...], lower[...]], axis=0)
    body = (parcel.shape[0] - code_rows) // WINDOW * WINDOW
    head = parcel.shape[0] - body
    blocks = [parcel[j : j + WINDOW] for j in range(head, head + body, WINDOW)]
    over = parcel[:head].T
    rows = jnp.concatenate([*blocks, over[:, code_rows:]], axis=1)
    total = None
    for w_gate, w_up, w_down in (weights[:3], weights[3:]):
        gate_val = jnp.dot(rows, w_gate[...], preferred_element_type=F32)
        up_val = jnp.dot(rows, w_up[...], preferred_element_type=F32)
        hidden = swiglu(gate_val, up_val).astype(BF16)
        term = jnp.dot(hidden, w_down[...], preferred_element_type=F32)
        total = term if total is None else total + term
    codes = over[:, :code_rows].astype(F32)
    mine = lax.broadcasted_iota(jnp.int32, codes.shape, 1) == place[0]
    code = jnp.sum(jnp.where(mine, codes, 0.0), axis=1, keepdims=True)
    terms = (total * (code / jnp.sum(codes, axis=1, keepdims=True))).astype(BF16)
    blocks = [terms[:, j : j + WINDOW] for j in range(0, body, WINDOW)]
    terms = jnp.concatenate([terms[:, body:].T, *blocks], axis=0)
    half = out_upper.shape[0]
    out_upper[...] = terms[:half]
    out_lower[...] = terms[half:]


def expert_terms(code_rows, expert, weights, parcel):
    half, rest = parcel[0].shape[0] - code_rows, parcel[1].shape[0]
    return pl.pallas_call(
        functools.partial(expert_kernel, code_rows),
        out_shape=[jax.ShapeDtypeStruct((n, WINDOW), BF16) for n in (half, rest)],
        in_specs=[SMEM] + [VMEM] * 8,
        out_specs=[VMEM] * 2,
        cost_estimate=pl.CostEstimate(flops=1, bytes_accessed=1, transcendentals=0),
        compiler_params=pltpu.CompilerParams(vmem_limit_bytes=24 * 2**20),
        name="experts",
    )(expert, *parcel, *weights)


def total_kernel(*refs):
    uppers, lowers, out = refs[:3], refs[3:6], refs[6]
    summed = [sum(ref[...].astype(F32) for ref in half) for half in (uppers, lowers)]
    summed = jnp.concatenate(summed, axis=0).astype(BF16)
    head = summed.shape[0] % WINDOW
    body = summed.shape[0] - head
    for j in range(0, body, WINDOW):
        out[j : j + WINDOW, :] = summed[head + j : head + j + WINDOW].T
    if head:
        out[body:, :] = summed[:head]


def total_of(uppers, lowers):
    features = uppers[0].shape[0] + lowers[0].shape[0]
    return pl.pallas_call(
        total_kernel,
        out_shape=jax.ShapeDtypeStruct((features, WINDOW), BF16),
        in_specs=[VMEM] * 6,
        out_specs=VMEM,
        cost_estimate=pl.CostEstimate(flops=1, bytes_accessed=1, transcendentals=0),
        compiler_params=pltpu.CompilerParams(vmem_limit_bytes=16 * 2**20),
        name="total",
    )(*uppers, *lowers)


def half_of(features):
    return features // 2 // BF16_ROWS * BF16_ROWS


def ring_of(count):
    order = list(range(0, count, 2)) + list(range(count - 1, 0, -2))
    right = [(order[i], order[(i + 1) % count]) for i in range(count)]
    return right, [(target, source) for source, target in right]


def add(a, b):
    return (a.astype(F32) + b.astype(F32)).astype(BF16)


def mixed_by_ring(parcel, code_rows, weights):
    count = lax.axis_size("seq")
    right, left = ring_of(count)
    far = count // 2
    expert = lax.axis_index("seq").astype(jnp.int32)[None]
    to_right = functools.partial(lax.ppermute, axis_name="seq", perm=right)
    to_left = functools.partial(lax.ppermute, axis_name="seq", perm=left)
    apply = functools.partial(expert_terms, code_rows, expert, weights)
    at = {0: parcel}
    at[-1], at[1] = [to_right(half) for half in parcel], [to_left(half) for half in parcel]
    terms = {}

    def work(k, arrived):
        at[k], arrived = after(at[k], arrived)
        terms[k] = apply(at[k])
        return arrived

    last = None
    for k in range(2, far + 1):
        uppers, lowers = (at[1 - k][0], at[k - 1][0]), (at[1 - k][1], at[k - 1][1])
        if last is not None:
            uppers, terms[last] = after(uppers, terms[last])
        upper_left = to_right(uppers[0])
        upper_right = to_left(uppers[1]) if k < far else None
        if k > 2:
            uppers = work(k - 2, uppers)
            lowers, terms[k - 2] = after(lowers, terms[k - 2])
        lower_left = to_right(lowers[0]) if k < far else None
        lower_right = to_left(lowers[1])
        at[1 - k], at[k - 1] = (uppers[0], lowers[0]), (uppers[1], lowers[1])
        if k < far:
            last = 1 - k
            terms[last] = apply(at[last])
        at[-k], at[k] = (upper_left, lower_left), (upper_right, lower_right)
    opposite = (at[-far][0], at[far][1])
    terms[far - 1] = apply(at[far - 1])
    right_low = to_right(terms[far - 1][1])
    terms[far - 1] = work(1 - far, terms[far - 1])
    left_up = to_left(terms[1 - far][0])
    opposite, terms[1 - far] = after(opposite, terms[1 - far])
    farthest = apply(opposite)
    farthest = work(0, farthest)
    right_up, left_low = to_right(farthest[0]), to_left(farthest[1])
    (left_up, right_low), terms[0] = after((left_up, right_low), terms[0])
    for k in range(far - 1, 0, -1):
        if k > 1:
            left_up = to_left(add(terms[1 - k][0], left_up))
            right_low = to_right(add(terms[k - 1][1], right_low))
        left_low = to_left(add(terms[-k][1], left_low))
        right_up = to_right(add(terms[k][0], right_up))
    near, final = after((terms[0], left_up, right_low), (left_low, right_up))
    (upper, lower), left_up, right_low = near
    left_low, right_up = final
    return total_of((upper, left_up, right_up), (lower, left_low, right_low))


def pack_rows(normed, expert_ids, gate_codes, expert_count, capacity):
    pair_ids = expert_ids.reshape(-1)
    matches = (pair_ids[:, None] == jnp.arange(expert_count, dtype=jnp.int32)[None, :]).astype(
        jnp.int32
    )
    within = jnp.sum((jnp.cumsum(matches, axis=0) - 1) * matches, axis=1)
    sources = normed[jnp.arange(pair_ids.shape[0], dtype=jnp.int32) // expert_ids.shape[1]]
    outbox = jnp.zeros((expert_count * capacity, normed.shape[1]), normed.dtype)
    outbox = outbox.at[pair_ids * capacity + within].set(sources)
    code_vals = gate_codes.astype(F32)
    shares = (code_vals / jnp.sum(code_vals, axis=1, keepdims=True)).reshape(-1)
    return (outbox, pair_ids, within, shares)


def mixed_by_packing(normed, routes, gate_codes, weights, expert_count, capacity):
    w_gate, w_up, w_down = weights
    owners, block = lax.axis_size("exp"), normed.shape[0]
    owner_pos = lax.axis_index("exp")
    own = lambda value: lax.dynamic_slice_in_dim(value, owner_pos * block, block, 0)
    outbox, pair_ids, within, shares = pack_rows(
        normed, own(routes), own(gate_codes), expert_count, capacity
    )
    outbox = outbox.reshape(expert_count, capacity, normed.shape[1])
    exchange = functools.partial(lax.all_to_all, axis_name="seq", split_axis=0, concat_axis=0, tiled=True)
    arrived = lax.all_gather(exchange(outbox), "exp", axis=0, tiled=True)
    flat_rows = arrived.reshape(-1, arrived.shape[-1])
    gate_val = jnp.dot(flat_rows, w_gate, preferred_element_type=F32)
    up_val = jnp.dot(flat_rows, w_up, preferred_element_type=F32)
    hidden = swiglu(gate_val, up_val).astype(BF16)
    partial_value = jnp.dot(hidden, w_down, preferred_element_type=F32).reshape(arrived.shape)
    whole = lax.psum_scatter(partial_value.astype(BF16), "exp", scatter_dimension=0, tiled=True)
    picked = exchange(whole)[pair_ids, within].astype(F32)
    mixture = jnp.sum((picked * shares[:, None]).reshape(-1, TOP, normed.shape[1]), axis=1)
    return mixture.astype(BF16)


def local(
    queries,
    key_rows,
    values,
    sink_logit,
    o_weight,
    residual,
    norm_gain,
    routes,
    gate_codes,
    w_gate,
    w_up,
    w_down,
):
    block_rows = residual.shape[0] // lax.axis_size("exp")
    expert_count = w_gate.shape[0] * lax.axis_size("seq")
    capacity = max(2, 2 * block_rows * TOP // expert_count)
    weights = (w_gate[0], w_up[0], w_down[0])
    attention = (queries, key_rows, values, sink_logit, o_weight, residual, norm_gain, routes, gate_codes)
    if capacity < block_rows:
        (attended,), weights = front(0, *attention, weights)
        attended = attended.T
        normed = rms_norm(attended, norm_gain)
        return (attended, mixed_by_packing(normed, routes, gate_codes, weights, expert_count, capacity))
    code_rows = -(-expert_count // BF16_ROWS) * BF16_ROWS
    (attended, *parcel), weights = front(code_rows, *attention, weights)
    gate_b, up_b = swapped(weights[0]), swapped(weights[1])
    down, parcel = after(weights[2], parcel)
    down_b = swapped(down)
    weights = [in_vmem(weight) for weight in (*weights, gate_b, up_b, down_b)]
    return (attended.T, mixed_by_ring(parcel, code_rows, weights).T)


def solution(mesh):
    placed = (
        P(("groups", "seq"), "exp"),
        P(("groups", "seq"), "exp"),
        P(("groups", "seq"), "exp"),
        P("exp"),
        P("exp", None),
        P(("groups", "seq"), None),
        P(),
        P(("groups", "seq"), None),
        P(("groups", "seq"), None),
        P("seq", None, "exp"),
        P("seq", None, "exp"),
        P("seq", "exp", None),
    )
    return jax.shard_map(
        local,
        mesh=mesh,
        in_specs=placed,
        out_specs=(P(("groups", "seq", "exp"), None), P(("groups", "seq", "exp"), None)),
        check_vma=False,
    )
```

```python
import functools

import jax
import jax.numpy as jnp
from jax import lax
from jax.experimental import pallas as pl
from jax.experimental.pallas import tpu as pltpu
from jax.sharding import PartitionSpec as P

HEAD_DIM = 64
WINDOW = 128
TOP = 4
BF16_ROWS = 16
F32 = jnp.float32
BF16 = jnp.bfloat16
VMEM = pl.BlockSpec(memory_space=pltpu.VMEM)
SMEM = pl.BlockSpec(memory_space=pltpu.SMEM)
ANY = pl.BlockSpec(memory_space=pl.ANY)
in_hbm = functools.partial(pltpu.with_memory_space_constraint, memory_space=pltpu.HBM)
in_vmem = functools.partial(pltpu.with_memory_space_constraint, memory_space=pltpu.VMEM)


def swiglu(gate_val, up_val):
    return (up_val + 1.0) * gate_val * jax.nn.sigmoid(1.702 * gate_val)


def heads_of(q_cols, past, present, sinks, first):
    kv_width = past.shape[1] // 2
    group = q_cols.shape[0] // kv_width
    shape = (WINDOW, group * WINDOW)
    query_at = lax.rem(lax.broadcasted_iota(jnp.int32, shape, 1), WINDOW)
    earlier = lax.broadcasted_iota(jnp.int32, shape, 0) > query_at
    both = jnp.concatenate([past, present], axis=0)
    outs = []
    for g in range(kv_width // HEAD_DIM):
        keys = both[:, g * HEAD_DIM : (g + 1) * HEAD_DIM]
        vals = both[:, kv_width + g * HEAD_DIM : kv_width + (g + 1) * HEAD_DIM].T
        heads = range(g * group, (g + 1) * group)
        q_group = jnp.concatenate([q_cols[h * HEAD_DIM : (h + 1) * HEAD_DIM] for h in heads], axis=1)
        scores = jnp.dot(keys, q_group, preferred_element_type=F32)
        seen = jnp.where(earlier, jnp.where(first, -1e30, scores[:WINDOW]), scores[WINDOW:])
        sink = jnp.concatenate([jnp.broadcast_to(sinks[:, h : h + 1], (1, WINDOW)) for h in heads], axis=1)
        ceiling = jnp.maximum(jnp.max(seen, axis=0, keepdims=True), sink)
        raised = jnp.exp(seen - ceiling)
        total = jnp.sum(raised, axis=0, keepdims=True) + jnp.exp(sink - ceiling)
        spread = jnp.concatenate([jnp.where(earlier, raised, 0.0), jnp.where(earlier, 0.0, raised)], axis=0)
        mixed = jnp.dot(vals, spread.astype(BF16), preferred_element_type=F32) * (1.0 / total)
        mixed = mixed.astype(BF16)
        outs += [mixed[:, i * WINDOW : (i + 1) * WINDOW] for i in range(group)]
    return jnp.concatenate(outs, axis=0)


def pack_kernel(code_rows, place, sink, gain, routes, codes, k, v, q, packed, *refs):
    *extra, sems = refs
    count, width = k.shape
    base = 2 * count + BF16_ROWS
    rows = pl.ds(pl.multiple_of(place[0] * WINDOW, WINDOW), WINDOW)
    others = pl.ds(pl.multiple_of((1 - place[0]) * WINDOW, WINDOW), WINDOW)
    moves = [(k, packed.at[:count, :]), (v, packed.at[count : 2 * count, :])]
    for j in range(q.shape[1] // width):
        to = base + j * WINDOW
        moves.append((q.at[others, j * width : (j + 1) * width], packed.at[to : to + WINDOW, :]))
    copies = [pltpu.make_async_copy(source, target, sems.at[i]) for i, (source, target) in enumerate(moves)]
    for copy in copies:
        copy.start()
    shape = (BF16_ROWS, width)
    lane, row = (lax.broadcasted_iota(jnp.int32, shape, i) for i in (1, 0))
    left = jnp.zeros(shape, F32)
    for h in range(sink.shape[0]):
        left = jnp.where(lane == h, sink[h], left)
    terms = jnp.zeros(shape, F32)
    for i in range(3):
        term = left.astype(BF16).astype(F32)
        terms = jnp.where(row == i, term, terms)
        left = left - term
    packed[2 * count : base, :] = terms.astype(BF16)
    if code_rows:
        gains, table_ref = extra
        gains[...] = jnp.broadcast_to(gain[...], (WINDOW, gain.shape[1])).T
        expert = lax.broadcasted_iota(jnp.int32, (code_rows, WINDOW), 0)
        table = jnp.zeros((code_rows, WINDOW), F32)
        for i in range(TOP):
            named = jnp.broadcast_to(routes[i : i + 1, rows], expert.shape) == expert
            table += jnp.where(named, jnp.broadcast_to(codes[i : i + 1, rows], expert.shape).astype(F32), 0.0)
        table_ref[...] = table.astype(BF16)
    for copy in copies:
        copy.wait()


def pack(code_rows, place, sink_logit, norm_gain, routes, gate_codes, key_rows, values, queries):
    rows, width = key_rows.shape
    tall = queries.shape[1] // width * WINDOW
    shapes = [jax.ShapeDtypeStruct((2 * rows + BF16_ROWS + tall, width), BF16)]
    if code_rows:
        features = norm_gain.shape[0]
        shapes += [jax.ShapeDtypeStruct((features, WINDOW), F32), jax.ShapeDtypeStruct((code_rows, WINDOW), BF16)]
    return pl.pallas_call(
        functools.partial(pack_kernel, code_rows),
        out_shape=shapes,
        in_specs=[SMEM] * 2 + [VMEM] * 3 + [ANY] * 3,
        out_specs=[VMEM] * len(shapes),
        scratch_shapes=[pltpu.SemaphoreType.DMA((2 + tall // WINDOW,))],
        cost_estimate=pl.CostEstimate(flops=1, bytes_accessed=1, transcendentals=0),
        compiler_params=pltpu.CompilerParams(vmem_limit_bytes=16 * 2**20),
        name="pack",
    )(
        place, in_hbm(sink_logit), norm_gain[None, :], in_hbm(routes.T), in_hbm(gate_codes.T),
        in_hbm(key_rows), in_hbm(values), in_hbm(queries),
    )


def rim_kernel(k, v, rim, sems):
    last = k.shape[0] - WINDOW
    copies = [
        pltpu.make_async_copy(k.at[last:, :], rim.at[:WINDOW, :], sems.at[0]),
        pltpu.make_async_copy(v.at[last:, :], rim.at[WINDOW:, :], sems.at[1]),
    ]
    for copy in copies:
        copy.start()
    for copy in copies:
        copy.wait()


def pack_rim(key_rows, values):
    return pl.pallas_call(
        rim_kernel,
        out_shape=jax.ShapeDtypeStruct((2 * WINDOW, key_rows.shape[1]), BF16),
        in_specs=[ANY, ANY],
        out_specs=VMEM,
        scratch_shapes=[pltpu.SemaphoreType.DMA((2,))],
        cost_estimate=pl.CostEstimate(flops=0, bytes_accessed=4 * key_rows.size, transcendentals=0),
        compiler_params=pltpu.CompilerParams(vmem_limit_bytes=4 * 2**20),
        name="rim",
    )(in_hbm(key_rows), in_hbm(values))


def attend(place, packed, rim, q_blocks):
    core, first = place[0], place[1] == 1
    start = pl.multiple_of(core * WINDOW, WINDOW)
    lead = core == 0
    tall = q_blocks.shape[0]
    base = packed.shape[0] - tall
    count = (base - BF16_ROWS) // 2
    past = jnp.concatenate(
        [
            jnp.where(lead, rim[:WINDOW, :], packed[:WINDOW, :]),
            jnp.where(lead, rim[WINDOW:, :], packed[count : count + WINDOW, :]),
        ],
        axis=1,
    )
    later = pl.ds(pl.multiple_of(count + start, WINDOW), WINDOW)
    present = jnp.concatenate([packed[pl.ds(start, WINDOW), :], packed[later, :]], axis=1)
    terms = packed[2 * count : base, :].astype(F32)
    sinks = terms[0:1] + terms[1:2] + terms[2:3]
    q_cols = [(q_blocks[j : j + WINDOW] * HEAD_DIM ** (-0.5)).T for j in range(0, tall, WINDOW)]
    return heads_of(jnp.concatenate(q_cols, axis=0), past, present, sinks, first)


def front_own_kernel(place, packed, rim, q, ow, resid, out, q_held, ow_held, resid_held, sems):
    rows = pl.ds(pl.multiple_of(place[0] * WINDOW, WINDOW), WINDOW)
    width = packed.shape[1]
    moves = [
        (q.at[rows, j * width : (j + 1) * width], q_held.at[j * WINDOW : (j + 1) * WINDOW, :])
        for j in range(q.shape[1] // width)
    ]
    moves += [(ow, ow_held), (resid.at[:, rows], resid_held)]
    copies = [pltpu.make_async_copy(source, target, sems.at[i]) for i, (source, target) in enumerate(moves)]
    for copy in copies:
        copy.start()
    for copy in copies[:-2]:
        copy.wait()
    heads = attend(place, packed, rim, q_held[...])
    for copy in copies[-2:]:
        copy.wait()
    projected = jnp.dot(ow_held[...], heads, preferred_element_type=F32)
    out[...] = projected + resid_held[...].astype(F32)


def front_kernel(code_rows, place, packed, rim, ow, stream, *refs):
    base = packed.shape[0] - ow.shape[1] // packed.shape[1] * WINDOW
    heads = attend(place, packed, rim, packed[base:, :])
    attended = (stream[...] + jnp.dot(ow[...], heads, preferred_element_type=F32)).astype(BF16)
    if not code_rows:
        refs[0][...] = attended
        return
    gains, table, attended_ref, upper, lower = refs
    attended_ref[...] = attended
    widened = attended.astype(F32)
    spread = jnp.mean(widened * widened, axis=0, keepdims=True)
    normed = (widened * lax.rsqrt(spread + 1e-05) * gains[...]).astype(BF16)
    body = normed.shape[0] // WINDOW * WINDOW
    blocks = [normed[j : j + WINDOW].T for j in range(0, body, WINDOW)]
    parcel = jnp.concatenate([table[...], normed[body:], *blocks], axis=0)
    upper[...] = parcel[: upper.shape[0]]
    lower[...] = parcel[upper.shape[0] :]


def front(code_rows, queries, key_rows, values, sink_logit, o_weight, residual, norm_gain, routes, gate_codes, weights):
    seq, core = lax.axis_index("seq"), lax.axis_index("exp")
    place = jnp.stack([core, jnp.where((seq == 0) & (core == 0), 1, 0)]).astype(jnp.int32)
    ow_b = swapped(o_weight.T)
    steps = [(s, s + 1) for s in range(lax.axis_size("seq") - 1)]
    rim_a = lax.ppermute(pack_rim(key_rows, values), "seq", steps)
    packed, *extra = pack(
        code_rows, place, sink_logit, norm_gain, routes, gate_codes, key_rows, values, queries
    )
    packed, rim_a = after(packed, rim_a)
    packed_b, rim_b = swapped(packed), swapped(rim_a)
    weights, rim_a = after(weights, rim_a)
    features = residual.shape[1]
    half = half_of(features)
    blocks = queries.shape[1] // packed.shape[1]
    held = ((blocks * WINDOW, packed.shape[1]), o_weight.T.shape, (features, WINDOW))
    cost = pl.CostEstimate(flops=1, bytes_accessed=1, transcendentals=0)
    params = pltpu.CompilerParams(vmem_limit_bytes=20 * 2**20)
    stream = pl.pallas_call(
        front_own_kernel,
        out_shape=jax.ShapeDtypeStruct((features, WINDOW), F32),
        in_specs=[SMEM] + [VMEM] * 2 + [ANY] * 3,
        out_specs=VMEM,
        scratch_shapes=[pltpu.VMEM(shape, BF16) for shape in held] + [pltpu.SemaphoreType.DMA((blocks + 2,))],
        cost_estimate=cost,
        compiler_params=params,
        name="front_own",
    )(place, packed, rim_a, in_hbm(queries), in_hbm(o_weight.T), in_hbm(residual.T))
    shapes = [(features, WINDOW)]
    if code_rows:
        shapes += [(code_rows + half, WINDOW), (features - half, WINDOW)]
    outs = pl.pallas_call(
        functools.partial(front_kernel, code_rows),
        out_shape=[jax.ShapeDtypeStruct(shape, BF16) for shape in shapes],
        in_specs=[SMEM] + [VMEM] * (4 + len(extra)),
        out_specs=[VMEM] * len(shapes),
        cost_estimate=cost,
        compiler_params=params,
        name="front",
    )(place, packed_b, rim_b, in_vmem(ow_b), stream, *extra)
    return outs, weights


def swapped(value):
    return lax.ppermute(value, "exp", [(0, 1), (1, 0)])


def after(value, earlier):
    return lax.optimization_barrier((value, earlier))


def rms_norm(stream, norm_gain):
    widened = stream.astype(F32)
    spread = jnp.mean(widened * widened, axis=-1, keepdims=True)
    return (widened * lax.rsqrt(spread + 1e-05) * norm_gain).astype(BF16)


def expert_kernel(code_rows, place, upper, lower, *refs):
    weights, more, (out_upper, out_lower) = refs[:6], refs[6:-2], refs[-2:]
    parcel = jnp.concatenate([upper[...], lower[...]], axis=0)
    body = (parcel.shape[0] - code_rows) // WINDOW * WINDOW
    head = parcel.shape[0] - body
    blocks = [parcel[j : j + WINDOW] for j in range(head, head + body, WINDOW)]
    over = parcel[:head].T
    rows = jnp.concatenate([*blocks, over[:, code_rows:]], axis=1)
    total = None
    for w_gate, w_up, w_down in (weights[:3], weights[3:]):
        gate_val = jnp.dot(rows, w_gate[...], preferred_element_type=F32)
        up_val = jnp.dot(rows, w_up[...], preferred_element_type=F32)
        hidden = swiglu(gate_val, up_val).astype(BF16)
        term = jnp.dot(hidden, w_down[...], preferred_element_type=F32)
        total = term if total is None else total + term
    codes = over[:, :code_rows].astype(F32)
    mine = lax.broadcasted_iota(jnp.int32, codes.shape, 1) == place[0]
    code = jnp.sum(jnp.where(mine, codes, 0.0), axis=1, keepdims=True)
    terms = (total * (code / jnp.sum(codes, axis=1, keepdims=True))).astype(BF16)
    blocks = [terms[:, j : j + WINDOW] for j in range(0, body, WINDOW)]
    terms = jnp.concatenate([terms[:, body:].T, *blocks], axis=0)
    half = out_upper.shape[0]
    out_upper[...] = terms[:half]
    out_lower[...] = add(terms[half:], more[0][...]) if more else terms[half:]


def expert_terms(code_rows, expert, weights, parcel, *more):
    half, rest = parcel[0].shape[0] - code_rows, parcel[1].shape[0]
    return pl.pallas_call(
        functools.partial(expert_kernel, code_rows),
        out_shape=[jax.ShapeDtypeStruct((n, WINDOW), BF16) for n in (half, rest)],
        in_specs=[SMEM] + [VMEM] * (8 + len(more)),
        out_specs=[VMEM] * 2,
        cost_estimate=pl.CostEstimate(flops=1000000000, bytes_accessed=1, transcendentals=0),
        compiler_params=pltpu.CompilerParams(vmem_limit_bytes=24 * 2**20),
        name="experts",
    )(expert, *parcel, *weights, *more)


def total_kernel(*refs):
    uppers, lowers, out = refs[:3], refs[3:6], refs[6]
    summed = [sum(ref[...].astype(F32) for ref in half) for half in (uppers, lowers)]
    summed = jnp.concatenate(summed, axis=0).astype(BF16)
    head = summed.shape[0] % WINDOW
    body = summed.shape[0] - head
    for j in range(0, body, WINDOW):
        out[j : j + WINDOW, :] = summed[head + j : head + j + WINDOW].T
    if head:
        out[body:, :] = summed[:head]


def total_of(uppers, lowers):
    features = uppers[0].shape[0] + lowers[0].shape[0]
    return pl.pallas_call(
        total_kernel,
        out_shape=jax.ShapeDtypeStruct((features, WINDOW), BF16),
        in_specs=[VMEM] * 6,
        out_specs=VMEM,
        cost_estimate=pl.CostEstimate(flops=1, bytes_accessed=1, transcendentals=0),
        compiler_params=pltpu.CompilerParams(vmem_limit_bytes=16 * 2**20),
        name="total",
    )(*uppers, *lowers)


def half_of(features):
    return features // 2 // BF16_ROWS * BF16_ROWS


def ring_of(count, cores):
    order = list(range(0, count, 2)) + list(range(count - 1, 0, -2))
    right = [(order[i], order[(i + 1) % count], core) for i in range(count) for core in range(cores)]
    steps = [(s * cores + c, t * cores + c) if c % 2 == 0 else (t * cores + c, s * cores + c) for s, t, c in right]
    return steps, [(target, source) for source, target in steps]


def add(a, b):
    return (a.astype(F32) + b.astype(F32)).astype(BF16)


def mixed_by_ring(parcel, code_rows, weights):
    count = lax.axis_size("seq")
    right, left = ring_of(count, lax.axis_size("exp"))
    far = count // 2
    expert = lax.axis_index("seq").astype(jnp.int32)[None]
    to_right = functools.partial(lax.ppermute, axis_name=("seq", "exp"), perm=right)
    to_left = functools.partial(lax.ppermute, axis_name=("seq", "exp"), perm=left)
    apply = functools.partial(expert_terms, code_rows, expert, weights)
    at = {0: parcel}
    at[-1], at[1] = [to_right(half) for half in parcel], [to_left(half) for half in parcel]
    terms = {}

    def work(k, arrived, *more):
        at[k], arrived = after(at[k], arrived)
        terms[k] = apply(at[k], *more)
        return arrived

    last = None
    last = 0
    terms[0] = apply(parcel)
    for k in range(2, far + 1):
        uppers, lowers = (at[1 - k][0], at[k - 1][0]), (at[1 - k][1], at[k - 1][1])
        if last is not None:
            uppers, terms[last] = after(uppers, terms[last])
        upper_left = to_right(uppers[0])
        upper_right = to_left(uppers[1]) if k < far else None
        if 2 < k == far:
            uppers = work(k - 2, uppers)
            lowers, terms[k - 2] = after(lowers, terms[k - 2])
        lower_left = to_right(lowers[0]) if k < far else None
        lower_right = to_left(lowers[1])
        at[1 - k], at[k - 1] = (uppers[0], lowers[0]), (uppers[1], lowers[1])
        if k < far:
            last = 1 - k
            terms[last] = apply(at[last])
        at[-k], at[k] = (upper_left, lower_left), (upper_right, lower_right)
    opposite = (at[-far][0], at[far][1])
    terms[far - 1] = apply(at[far - 1])
    right_low = to_right(terms[far - 1][1])
    terms[far - 1] = work(1 - far, terms[far - 1])
    left_up = to_left(terms[1 - far][0])
    opposite, terms[1 - far] = after(opposite, terms[1 - far])
    farthest = apply(opposite)
    right_up, left_low = to_right(farthest[0]), to_left(farthest[1])
    fused = False
    farthest = work(1, farthest)
    right_low, terms[1] = after(right_low, terms[1])
    left_up, terms[1] = after(left_up, terms[1])
    for k in range(far - 1, 0, -1):
        if k > 1:
            going = terms[k - 1][1]
            if not fused:
                going = add(going, right_low)
            fused = False
            right_low = to_right(going)
            left_up = to_left(add(terms[1 - k][0], left_up))
        right_up = to_right(add(terms[k][0], right_up))
        left_low = to_left(add(terms[-k][1], left_low))
    near, final = after((terms[0], left_up, right_low), (left_low, right_up))
    (upper, lower), left_up, right_low = near
    left_low, right_up = final
    return total_of((upper, left_up, right_up), (lower, left_low, right_low))


def pack_rows(normed, expert_ids, gate_codes, expert_count, capacity):
    pair_ids = expert_ids.reshape(-1)
    matches = (pair_ids[:, None] == jnp.arange(expert_count, dtype=jnp.int32)[None, :]).astype(
        jnp.int32
    )
    within = jnp.sum((jnp.cumsum(matches, axis=0) - 1) * matches, axis=1)
    sources = normed[jnp.arange(pair_ids.shape[0], dtype=jnp.int32) // expert_ids.shape[1]]
    outbox = jnp.zeros((expert_count * capacity, normed.shape[1]), normed.dtype)
    outbox = outbox.at[pair_ids * capacity + within].set(sources)
    code_vals = gate_codes.astype(F32)
    shares = (code_vals / jnp.sum(code_vals, axis=1, keepdims=True)).reshape(-1)
    return (outbox, pair_ids, within, shares)


def mixed_by_packing(normed, routes, gate_codes, weights, expert_count, capacity):
    w_gate, w_up, w_down = weights
    owners, block = lax.axis_size("exp"), normed.shape[0]
    owner_pos = lax.axis_index("exp")
    own = lambda value: lax.dynamic_slice_in_dim(value, owner_pos * block, block, 0)
    outbox, pair_ids, within, shares = pack_rows(
        normed, own(routes), own(gate_codes), expert_count, capacity
    )
    outbox = outbox.reshape(expert_count, capacity, normed.shape[1])
    exchange = functools.partial(lax.all_to_all, axis_name="seq", split_axis=0, concat_axis=0, tiled=True)
    arrived = lax.all_gather(exchange(outbox), "exp", axis=0, tiled=True)
    flat_rows = arrived.reshape(-1, arrived.shape[-1])
    gate_val = jnp.dot(flat_rows, w_gate, preferred_element_type=F32)
    up_val = jnp.dot(flat_rows, w_up, preferred_element_type=F32)
    hidden = swiglu(gate_val, up_val).astype(BF16)
    partial_value = jnp.dot(hidden, w_down, preferred_element_type=F32).reshape(arrived.shape)
    whole = lax.psum_scatter(partial_value.astype(BF16), "exp", scatter_dimension=0, tiled=True)
    picked = exchange(whole)[pair_ids, within].astype(F32)
    mixture = jnp.sum((picked * shares[:, None]).reshape(-1, TOP, normed.shape[1]), axis=1)
    return mixture.astype(BF16)


def local(
    queries,
    key_rows,
    values,
    sink_logit,
    o_weight,
    residual,
    norm_gain,
    routes,
    gate_codes,
    w_gate,
    w_up,
    w_down,
):
    block_rows = residual.shape[0] // lax.axis_size("exp")
    expert_count = w_gate.shape[0] * lax.axis_size("seq")
    capacity = max(2, 2 * block_rows * TOP // expert_count)
    weights = (w_gate[0], w_up[0], w_down[0])
    attention = (queries, key_rows, values, sink_logit, o_weight, residual, norm_gain, routes, gate_codes)
    if capacity < block_rows:
        (attended,), weights = front(0, *attention, weights)
        attended = attended.T
        normed = rms_norm(attended, norm_gain)
        return (attended, mixed_by_packing(normed, routes, gate_codes, weights, expert_count, capacity))
    code_rows = -(-expert_count // BF16_ROWS) * BF16_ROWS
    (attended, *parcel), weights = front(code_rows, *attention, weights)
    gate_b, up_b = swapped(weights[0]), swapped(weights[1])
    down, parcel = after(weights[2], parcel)
    down_b = swapped(down)
    weights = [in_vmem(weight) for weight in (*weights, gate_b, up_b, down_b)]
    return (attended.T, mixed_by_ring(parcel, code_rows, weights).T)


def solution(mesh):
    placed = (
        P(("groups", "seq"), "exp"),
        P(("groups", "seq"), "exp"),
        P(("groups", "seq"), "exp"),
        P("exp"),
        P("exp", None),
        P(("groups", "seq"), None),
        P(),
        P(("groups", "seq"), None),
        P(("groups", "seq"), None),
        P("seq", None, "exp"),
        P("seq", None, "exp"),
        P("seq", "exp", None),
    )
    return jax.shard_map(
        local,
        mesh=mesh,
        in_specs=placed,
        out_specs=(P(("groups", "seq", "exp"), None), P(("groups", "seq", "exp"), None)),
        check_vma=False,
    )
```

```python
import functools

import jax
import jax.numpy as jnp
from jax import lax
from jax.experimental import pallas as pl
from jax.experimental.pallas import tpu as pltpu
from jax.sharding import PartitionSpec as P

HEAD_DIM = 64
WINDOW = 128
TOP = 4
BF16_ROWS = 16
F32 = jnp.float32
BF16 = jnp.bfloat16
VMEM = pl.BlockSpec(memory_space=pltpu.VMEM)
SMEM = pl.BlockSpec(memory_space=pltpu.SMEM)
ANY = pl.BlockSpec(memory_space=pl.ANY)
in_hbm = functools.partial(pltpu.with_memory_space_constraint, memory_space=pltpu.HBM)
in_vmem = functools.partial(pltpu.with_memory_space_constraint, memory_space=pltpu.VMEM)


def swiglu(gate_val, up_val):
    return (up_val + 1.0) * gate_val * jax.nn.sigmoid(1.702 * gate_val)


def heads_of(q_cols, past, present, sinks, first):
    kv_width = past.shape[1] // 2
    group = q_cols.shape[0] // kv_width
    shape = (WINDOW, group * WINDOW)
    query_at = lax.rem(lax.broadcasted_iota(jnp.int32, shape, 1), WINDOW)
    earlier = lax.broadcasted_iota(jnp.int32, shape, 0) > query_at
    both = jnp.concatenate([past, present], axis=0)
    outs = []
    for g in range(kv_width // HEAD_DIM):
        keys = both[:, g * HEAD_DIM : (g + 1) * HEAD_DIM]
        vals = both[:, kv_width + g * HEAD_DIM : kv_width + (g + 1) * HEAD_DIM].T
        heads = range(g * group, (g + 1) * group)
        q_group = jnp.concatenate([q_cols[h * HEAD_DIM : (h + 1) * HEAD_DIM] for h in heads], axis=1)
        scores = jnp.dot(keys, q_group, preferred_element_type=F32)
        seen = jnp.where(earlier, jnp.where(first, -1e30, scores[:WINDOW]), scores[WINDOW:])
        sink = jnp.concatenate([jnp.broadcast_to(sinks[:, h : h + 1], (1, WINDOW)) for h in heads], axis=1)
        ceiling = jnp.maximum(jnp.max(seen, axis=0, keepdims=True), sink)
        raised = jnp.exp(seen - ceiling)
        total = jnp.sum(raised, axis=0, keepdims=True) + jnp.exp(sink - ceiling)
        spread = jnp.concatenate([jnp.where(earlier, raised, 0.0), jnp.where(earlier, 0.0, raised)], axis=0)
        mixed = jnp.dot(vals, spread.astype(BF16), preferred_element_type=F32) * (1.0 / total)
        mixed = mixed.astype(BF16)
        outs += [mixed[:, i * WINDOW : (i + 1) * WINDOW] for i in range(group)]
    return jnp.concatenate(outs, axis=0)


def pack_kernel(code_rows, place, sink, gain, routes, codes, k, v, q, packed, *refs):
    *extra, sems = refs
    count, width = k.shape
    base = 2 * count + BF16_ROWS
    rows = pl.ds(pl.multiple_of(place[0] * WINDOW, WINDOW), WINDOW)
    others = pl.ds(pl.multiple_of((1 - place[0]) * WINDOW, WINDOW), WINDOW)
    moves = [(k, packed.at[:count, :]), (v, packed.at[count : 2 * count, :])]
    for j in range(q.shape[1] // width):
        to = base + j * WINDOW
        moves.append((q.at[others, j * width : (j + 1) * width], packed.at[to : to + WINDOW, :]))
    copies = [pltpu.make_async_copy(source, target, sems.at[i]) for i, (source, target) in enumerate(moves)]
    for copy in copies:
        copy.start()
    shape = (BF16_ROWS, width)
    lane, row = (lax.broadcasted_iota(jnp.int32, shape, i) for i in (1, 0))
    left = jnp.zeros(shape, F32)
    for h in range(sink.shape[0]):
        left = jnp.where(lane == h, sink[h], left)
    terms = jnp.zeros(shape, F32)
    for i in range(3):
        term = left.astype(BF16).astype(F32)
        terms = jnp.where(row == i, term, terms)
        left = left - term
    packed[2 * count : base, :] = terms.astype(BF16)
    if code_rows:
        gains, table_ref = extra
        gains[...] = jnp.broadcast_to(gain[...], (WINDOW, gain.shape[1])).T
        expert = lax.broadcasted_iota(jnp.int32, (code_rows, WINDOW), 0)
        table = jnp.zeros((code_rows, WINDOW), F32)
        for i in range(TOP):
            named = jnp.broadcast_to(routes[i : i + 1, rows], expert.shape) == expert
            table += jnp.where(named, jnp.broadcast_to(codes[i : i + 1, rows], expert.shape).astype(F32), 0.0)
        table_ref[...] = table.astype(BF16)
    for copy in copies:
        copy.wait()


def pack(code_rows, place, sink_logit, norm_gain, routes, gate_codes, key_rows, values, queries):
    rows, width = key_rows.shape
    tall = queries.shape[1] // width * WINDOW
    shapes = [jax.ShapeDtypeStruct((2 * rows + BF16_ROWS + tall, width), BF16)]
    if code_rows:
        features = norm_gain.shape[0]
        shapes += [jax.ShapeDtypeStruct((features, WINDOW), F32), jax.ShapeDtypeStruct((code_rows, WINDOW), BF16)]
    return pl.pallas_call(
        functools.partial(pack_kernel, code_rows),
        out_shape=shapes,
        in_specs=[SMEM] * 2 + [VMEM] * 3 + [ANY] * 3,
        out_specs=[VMEM] * len(shapes),
        scratch_shapes=[pltpu.SemaphoreType.DMA((2 + tall // WINDOW,))],
        cost_estimate=pl.CostEstimate(flops=1, bytes_accessed=1, transcendentals=0),
        compiler_params=pltpu.CompilerParams(vmem_limit_bytes=16 * 2**20),
        name="pack",
    )(
        place, in_hbm(sink_logit), norm_gain[None, :], in_hbm(routes.T), in_hbm(gate_codes.T),
        in_hbm(key_rows), in_hbm(values), in_hbm(queries),
    )


def rim_kernel(k, v, rim, sems):
    last = k.shape[0] - WINDOW
    copies = [
        pltpu.make_async_copy(k.at[last:, :], rim.at[:WINDOW, :], sems.at[0]),
        pltpu.make_async_copy(v.at[last:, :], rim.at[WINDOW:, :], sems.at[1]),
    ]
    for copy in copies:
        copy.start()
    for copy in copies:
        copy.wait()


def pack_rim(key_rows, values):
    return pl.pallas_call(
        rim_kernel,
        out_shape=jax.ShapeDtypeStruct((2 * WINDOW, key_rows.shape[1]), BF16),
        in_specs=[ANY, ANY],
        out_specs=VMEM,
        scratch_shapes=[pltpu.SemaphoreType.DMA((2,))],
        cost_estimate=pl.CostEstimate(flops=0, bytes_accessed=4 * key_rows.size, transcendentals=0),
        compiler_params=pltpu.CompilerParams(vmem_limit_bytes=4 * 2**20),
        name="rim",
    )(in_hbm(key_rows), in_hbm(values))


def attend(place, packed, rim, q_blocks):
    core, first = place[0], place[1] == 1
    start = pl.multiple_of(core * WINDOW, WINDOW)
    lead = core == 0
    tall = q_blocks.shape[0]
    base = packed.shape[0] - tall
    count = (base - BF16_ROWS) // 2
    past = jnp.concatenate(
        [
            jnp.where(lead, rim[:WINDOW, :], packed[:WINDOW, :]),
            jnp.where(lead, rim[WINDOW:, :], packed[count : count + WINDOW, :]),
        ],
        axis=1,
    )
    later = pl.ds(pl.multiple_of(count + start, WINDOW), WINDOW)
    present = jnp.concatenate([packed[pl.ds(start, WINDOW), :], packed[later, :]], axis=1)
    terms = packed[2 * count : base, :].astype(F32)
    sinks = terms[0:1] + terms[1:2] + terms[2:3]
    q_cols = [(q_blocks[j : j + WINDOW] * HEAD_DIM ** (-0.5)).T for j in range(0, tall, WINDOW)]
    return heads_of(jnp.concatenate(q_cols, axis=0), past, present, sinks, first)


def front_own_kernel(place, packed, rim, q, ow, resid, out, q_held, ow_held, resid_held, sems):
    rows = pl.ds(pl.multiple_of(place[0] * WINDOW, WINDOW), WINDOW)
    width = packed.shape[1]
    moves = [
        (q.at[rows, j * width : (j + 1) * width], q_held.at[j * WINDOW : (j + 1) * WINDOW, :])
        for j in range(q.shape[1] // width)
    ]
    moves += [(ow, ow_held), (resid.at[:, rows], resid_held)]
    copies = [pltpu.make_async_copy(source, target, sems.at[i]) for i, (source, target) in enumerate(moves)]
    for copy in copies:
        copy.start()
    for copy in copies[:-2]:
        copy.wait()
    heads = attend(place, packed, rim, q_held[...])
    for copy in copies[-2:]:
        copy.wait()
    projected = jnp.dot(ow_held[...], heads, preferred_element_type=F32)
    out[...] = projected + resid_held[...].astype(F32)


def front_kernel(code_rows, place, packed, rim, ow, stream, *refs):
    base = packed.shape[0] - ow.shape[1] // packed.shape[1] * WINDOW
    heads = attend(place, packed, rim, packed[base:, :])
    attended = (stream[...] + jnp.dot(ow[...], heads, preferred_element_type=F32)).astype(BF16)
    if not code_rows:
        refs[0][...] = attended
        return
    gains, table, attended_ref, upper, lower = refs
    attended_ref[...] = attended
    widened = attended.astype(F32)
    spread = jnp.mean(widened * widened, axis=0, keepdims=True)
    normed = (widened * lax.rsqrt(spread + 1e-05) * gains[...]).astype(BF16)
    body = normed.shape[0] // WINDOW * WINDOW
    blocks = [normed[j : j + WINDOW].T for j in range(0, body, WINDOW)]
    parcel = jnp.concatenate([table[...], normed[body:], *blocks], axis=0)
    upper[...] = parcel[: upper.shape[0]]
    lower[...] = parcel[upper.shape[0] :]


def front(code_rows, queries, key_rows, values, sink_logit, o_weight, residual, norm_gain, routes, gate_codes, weights):
    seq, core = lax.axis_index("seq"), lax.axis_index("exp")
    place = jnp.stack([core, jnp.where((seq == 0) & (core == 0), 1, 0)]).astype(jnp.int32)
    ow_b = swapped(o_weight.T)
    steps = [(s, s + 1) for s in range(lax.axis_size("seq") - 1)]
    rim_a = lax.ppermute(pack_rim(key_rows, values), "seq", steps)
    packed, *extra = pack(
        code_rows, place, sink_logit, norm_gain, routes, gate_codes, key_rows, values, queries
    )
    packed, rim_a = after(packed, rim_a)
    packed_b, rim_b = swapped(packed), swapped(rim_a)
    weights, rim_a = after(weights, rim_a)
    features = residual.shape[1]
    half = half_of(features)
    blocks = queries.shape[1] // packed.shape[1]
    held = ((blocks * WINDOW, packed.shape[1]), o_weight.T.shape, (features, WINDOW))
    cost = pl.CostEstimate(flops=1, bytes_accessed=1, transcendentals=0)
    params = pltpu.CompilerParams(vmem_limit_bytes=20 * 2**20)
    stream = pl.pallas_call(
        front_own_kernel,
        out_shape=jax.ShapeDtypeStruct((features, WINDOW), F32),
        in_specs=[SMEM] + [VMEM] * 2 + [ANY] * 3,
        out_specs=VMEM,
        scratch_shapes=[pltpu.VMEM(shape, BF16) for shape in held] + [pltpu.SemaphoreType.DMA((blocks + 2,))],
        cost_estimate=cost,
        compiler_params=params,
        name="front_own",
    )(place, packed, rim_a, in_hbm(queries), in_hbm(o_weight.T), in_hbm(residual.T))
    shapes = [(features, WINDOW)]
    if code_rows:
        shapes += [(code_rows + half, WINDOW), (features - half, WINDOW)]
    outs = pl.pallas_call(
        functools.partial(front_kernel, code_rows),
        out_shape=[jax.ShapeDtypeStruct(shape, BF16) for shape in shapes],
        in_specs=[SMEM] + [VMEM] * (4 + len(extra)),
        out_specs=[VMEM] * len(shapes),
        cost_estimate=cost,
        compiler_params=params,
        name="front",
    )(place, packed_b, rim_b, in_vmem(ow_b), stream, *extra)
    return outs, weights


def swapped(value):
    return lax.ppermute(value, "exp", [(0, 1), (1, 0)])


def after(value, earlier):
    return lax.optimization_barrier((value, earlier))


def rms_norm(stream, norm_gain):
    widened = stream.astype(F32)
    spread = jnp.mean(widened * widened, axis=-1, keepdims=True)
    return (widened * lax.rsqrt(spread + 1e-05) * norm_gain).astype(BF16)


def expert_kernel(code_rows, place, upper, lower, *refs):
    weights, (out_upper, out_lower) = refs[:6], refs[6:]
    parcel = jnp.concatenate([upper[...], lower[...]], axis=0)
    body = (parcel.shape[0] - code_rows) // WINDOW * WINDOW
    head = parcel.shape[0] - body
    blocks = [parcel[j : j + WINDOW] for j in range(head, head + body, WINDOW)]
    over = parcel[:head].T
    rows = jnp.concatenate([*blocks, over[:, code_rows:]], axis=1)
    total = None
    for w_gate, w_up, w_down in (weights[:3], weights[3:]):
        gate_val = jnp.dot(rows, w_gate[...], preferred_element_type=F32)
        up_val = jnp.dot(rows, w_up[...], preferred_element_type=F32)
        hidden = swiglu(gate_val, up_val).astype(BF16)
        term = jnp.dot(hidden, w_down[...], preferred_element_type=F32)
        total = term if total is None else total + term
    codes = over[:, :code_rows].astype(F32)
    mine = lax.broadcasted_iota(jnp.int32, codes.shape, 1) == place[0]
    code = jnp.sum(jnp.where(mine, codes, 0.0), axis=1, keepdims=True)
    terms = (total * (code / jnp.sum(codes, axis=1, keepdims=True))).astype(BF16)
    blocks = [terms[:, j : j + WINDOW] for j in range(0, body, WINDOW)]
    terms = jnp.concatenate([terms[:, body:].T, *blocks], axis=0)
    half = out_upper.shape[0]
    out_upper[...] = terms[:half]
    out_lower[...] = terms[half:]


def expert_terms(code_rows, expert, weights, parcel):
    half, rest = parcel[0].shape[0] - code_rows, parcel[1].shape[0]
    return pl.pallas_call(
        functools.partial(expert_kernel, code_rows),
        out_shape=[jax.ShapeDtypeStruct((n, WINDOW), BF16) for n in (half, rest)],
        in_specs=[SMEM] + [VMEM] * 8,
        out_specs=[VMEM] * 2,
        cost_estimate=pl.CostEstimate(flops=10**9, bytes_accessed=1, transcendentals=0),
        compiler_params=pltpu.CompilerParams(vmem_limit_bytes=24 * 2**20),
        name="experts",
    )(expert, *parcel, *weights)


def total_kernel(*refs):
    uppers, lowers, out = refs[:3], refs[3:6], refs[6]
    summed = [sum(ref[...].astype(F32) for ref in half) for half in (uppers, lowers)]
    summed = jnp.concatenate(summed, axis=0).astype(BF16)
    head = summed.shape[0] % WINDOW
    body = summed.shape[0] - head
    for j in range(0, body, WINDOW):
        out[j : j + WINDOW, :] = summed[head + j : head + j + WINDOW].T
    if head:
        out[body:, :] = summed[:head]


def total_of(uppers, lowers):
    features = uppers[0].shape[0] + lowers[0].shape[0]
    return pl.pallas_call(
        total_kernel,
        out_shape=jax.ShapeDtypeStruct((features, WINDOW), BF16),
        in_specs=[VMEM] * 6,
        out_specs=VMEM,
        cost_estimate=pl.CostEstimate(flops=1, bytes_accessed=1, transcendentals=0),
        compiler_params=pltpu.CompilerParams(vmem_limit_bytes=16 * 2**20),
        name="total",
    )(*uppers, *lowers)


def half_of(features):
    return features // 2 // BF16_ROWS * BF16_ROWS


def ring_of(count, cores):
    order = list(range(0, count, 2)) + list(range(count - 1, 0, -2))
    right = [(order[i], order[(i + 1) % count], core) for i in range(count) for core in range(cores)]
    steps = [(s * cores + c, t * cores + c) if c % 2 == 0 else (t * cores + c, s * cores + c) for s, t, c in right]
    return steps, [(target, source) for source, target in steps]


def add(a, b):
    return (a.astype(F32) + b.astype(F32)).astype(BF16)


def mixed_by_ring(parcel, code_rows, weights):
    count = lax.axis_size("seq")
    right, left = ring_of(count, lax.axis_size("exp"))
    far = count // 2
    expert = lax.axis_index("seq").astype(jnp.int32)[None]
    to_right = functools.partial(lax.ppermute, axis_name=("seq", "exp"), perm=right)
    to_left = functools.partial(lax.ppermute, axis_name=("seq", "exp"), perm=left)
    apply = functools.partial(expert_terms, code_rows, expert, weights)
    at = {0: parcel}
    at[-1], at[1] = [to_right(half) for half in parcel], [to_left(half) for half in parcel]
    terms = {}

    def work(k, arrived):
        at[k], arrived = after(at[k], arrived)
        terms[k] = apply(at[k])
        return arrived

    last = 0
    terms[0] = apply(parcel)
    for k in range(2, far + 1):
        uppers, lowers = (at[1 - k][0], at[k - 1][0]), (at[1 - k][1], at[k - 1][1])
        uppers, terms[last] = after(uppers, terms[last])
        upper_left = to_right(uppers[0])
        upper_right = to_left(uppers[1]) if k < far else None
        if 2 < k == far:
            uppers = work(k - 2, uppers)
            lowers, terms[k - 2] = after(lowers, terms[k - 2])
        lower_left = to_right(lowers[0]) if k < far else None
        lower_right = to_left(lowers[1])
        at[1 - k], at[k - 1] = (uppers[0], lowers[0]), (uppers[1], lowers[1])
        if k < far:
            last = 1 - k
            terms[last] = apply(at[last])
        at[-k], at[k] = (upper_left, lower_left), (upper_right, lower_right)
    opposite = (at[-far][0], at[far][1])
    terms[far - 1] = apply(at[far - 1])
    right_low = to_right(terms[far - 1][1])
    terms[far - 1] = work(1 - far, terms[far - 1])
    left_up = to_left(terms[1 - far][0])
    opposite, terms[1 - far] = after(opposite, terms[1 - far])
    farthest = apply(opposite)
    right_up, left_low = to_right(farthest[0]), to_left(farthest[1])
    for k in range(1, far - 2):
        farthest = work(k, farthest)
        (left_up, right_low), terms[k] = after((left_up, right_low), terms[k])
    for k in range(far - 1, 0, -1):
        right_up = to_right(add(terms[k][0], right_up))
        left_low = to_left(add(terms[-k][1], left_low))
        if k > 1:
            right_low = to_right(add(terms[k - 1][1], right_low))
            left_up = to_left(add(terms[1 - k][0], left_up))
    near, final = after((terms[0], left_up, right_low), (left_low, right_up))
    (upper, lower), left_up, right_low = near
    left_low, right_up = final
    return total_of((upper, left_up, right_up), (lower, left_low, right_low))


def pack_rows(normed, expert_ids, gate_codes, expert_count, capacity):
    pair_ids = expert_ids.reshape(-1)
    matches = (pair_ids[:, None] == jnp.arange(expert_count, dtype=jnp.int32)[None, :]).astype(
        jnp.int32
    )
    within = jnp.sum((jnp.cumsum(matches, axis=0) - 1) * matches, axis=1)
    sources = normed[jnp.arange(pair_ids.shape[0], dtype=jnp.int32) // expert_ids.shape[1]]
    outbox = jnp.zeros((expert_count * capacity, normed.shape[1]), normed.dtype)
    outbox = outbox.at[pair_ids * capacity + within].set(sources)
    code_vals = gate_codes.astype(F32)
    shares = (code_vals / jnp.sum(code_vals, axis=1, keepdims=True)).reshape(-1)
    return (outbox, pair_ids, within, shares)


def mixed_by_packing(normed, routes, gate_codes, weights, expert_count, capacity):
    w_gate, w_up, w_down = weights
    owners, block = lax.axis_size("exp"), normed.shape[0]
    owner_pos = lax.axis_index("exp")
    own = lambda value: lax.dynamic_slice_in_dim(value, owner_pos * block, block, 0)
    outbox, pair_ids, within, shares = pack_rows(
        normed, own(routes), own(gate_codes), expert_count, capacity
    )
    outbox = outbox.reshape(expert_count, capacity, normed.shape[1])
    exchange = functools.partial(lax.all_to_all, axis_name="seq", split_axis=0, concat_axis=0, tiled=True)
    arrived = lax.all_gather(exchange(outbox), "exp", axis=0, tiled=True)
    flat_rows = arrived.reshape(-1, arrived.shape[-1])
    gate_val = jnp.dot(flat_rows, w_gate, preferred_element_type=F32)
    up_val = jnp.dot(flat_rows, w_up, preferred_element_type=F32)
    hidden = swiglu(gate_val, up_val).astype(BF16)
    partial_value = jnp.dot(hidden, w_down, preferred_element_type=F32).reshape(arrived.shape)
    whole = lax.psum_scatter(partial_value.astype(BF16), "exp", scatter_dimension=0, tiled=True)
    picked = exchange(whole)[pair_ids, within].astype(F32)
    mixture = jnp.sum((picked * shares[:, None]).reshape(-1, TOP, normed.shape[1]), axis=1)
    return mixture.astype(BF16)


def local(
    queries,
    key_rows,
    values,
    sink_logit,
    o_weight,
    residual,
    norm_gain,
    routes,
    gate_codes,
    w_gate,
    w_up,
    w_down,
):
    block_rows = residual.shape[0] // lax.axis_size("exp")
    expert_count = w_gate.shape[0] * lax.axis_size("seq")
    capacity = max(2, 2 * block_rows * TOP // expert_count)
    weights = (w_gate[0], w_up[0], w_down[0])
    attention = (queries, key_rows, values, sink_logit, o_weight, residual, norm_gain, routes, gate_codes)
    if capacity < block_rows:
        (attended,), weights = front(0, *attention, weights)
        attended = attended.T
        normed = rms_norm(attended, norm_gain)
        return (attended, mixed_by_packing(normed, routes, gate_codes, weights, expert_count, capacity))
    code_rows = -(-expert_count // BF16_ROWS) * BF16_ROWS
    (attended, *parcel), weights = front(code_rows, *attention, weights)
    gate_b, up_b = swapped(weights[0]), swapped(weights[1])
    down, parcel = after(weights[2], parcel)
    down_b = swapped(down)
    weights = [in_vmem(weight) for weight in (*weights, gate_b, up_b, down_b)]
    return (attended.T, mixed_by_ring(parcel, code_rows, weights).T)


def solution(mesh):
    placed = (
        P(("groups", "seq"), "exp"),
        P(("groups", "seq"), "exp"),
        P(("groups", "seq"), "exp"),
        P("exp"),
        P("exp", None),
        P(("groups", "seq"), None),
        P(),
        P(("groups", "seq"), None),
        P(("groups", "seq"), None),
        P("seq", None, "exp"),
        P("seq", None, "exp"),
        P("seq", "exp", None),
    )
    return jax.shard_map(
        local,
        mesh=mesh,
        in_specs=placed,
        out_specs=(P(("groups", "seq", "exp"), None), P(("groups", "seq", "exp"), None)),
        check_vma=False,
    )
```

```python
import functools

import jax
import jax.numpy as jnp
from jax import lax
from jax.experimental import pallas as pl
from jax.experimental.pallas import tpu as pltpu
from jax.sharding import PartitionSpec as P

HEAD_DIM = 64
WINDOW = 128
TOP = 4
BF16_ROWS = 16
F32 = jnp.float32
BF16 = jnp.bfloat16
VMEM = pl.BlockSpec(memory_space=pltpu.VMEM)
SMEM = pl.BlockSpec(memory_space=pltpu.SMEM)
ANY = pl.BlockSpec(memory_space=pl.ANY)
in_hbm = functools.partial(pltpu.with_memory_space_constraint, memory_space=pltpu.HBM)
in_vmem = functools.partial(pltpu.with_memory_space_constraint, memory_space=pltpu.VMEM)


def swiglu(gate_val, up_val):
    return (up_val + 1.0) * gate_val * jax.nn.sigmoid(1.702 * gate_val)


def heads_of(q_cols, past, present, sinks, first):
    kv_width = past.shape[1] // 2
    group = q_cols.shape[0] // kv_width
    shape = (WINDOW, group * WINDOW)
    query_at = lax.rem(lax.broadcasted_iota(jnp.int32, shape, 1), WINDOW)
    earlier = lax.broadcasted_iota(jnp.int32, shape, 0) > query_at
    both = jnp.concatenate([past, present], axis=0)
    outs = []
    for g in range(kv_width // HEAD_DIM):
        keys = both[:, g * HEAD_DIM : (g + 1) * HEAD_DIM]
        vals = both[:, kv_width + g * HEAD_DIM : kv_width + (g + 1) * HEAD_DIM].T
        heads = range(g * group, (g + 1) * group)
        q_group = jnp.concatenate([q_cols[h * HEAD_DIM : (h + 1) * HEAD_DIM] for h in heads], axis=1)
        scores = jnp.dot(keys, q_group, preferred_element_type=F32)
        seen = jnp.where(earlier, jnp.where(first, -1e30, scores[:WINDOW]), scores[WINDOW:])
        sink = jnp.concatenate([jnp.broadcast_to(sinks[:, h : h + 1], (1, WINDOW)) for h in heads], axis=1)
        ceiling = jnp.maximum(jnp.max(seen, axis=0, keepdims=True), sink)
        raised = jnp.exp(seen - ceiling)
        total = jnp.sum(raised, axis=0, keepdims=True) + jnp.exp(sink - ceiling)
        spread = jnp.concatenate([jnp.where(earlier, raised, 0.0), jnp.where(earlier, 0.0, raised)], axis=0)
        mixed = jnp.dot(vals, spread.astype(BF16), preferred_element_type=F32) * (1.0 / total)
        mixed = mixed.astype(BF16)
        outs += [mixed[:, i * WINDOW : (i + 1) * WINDOW] for i in range(group)]
    return jnp.concatenate(outs, axis=0)


def pack_kernel(code_rows, place, sink, gain, routes, codes, k, v, q, packed, *refs):
    *extra, sems = refs
    count, width = k.shape
    base = 2 * count + BF16_ROWS
    rows = pl.ds(pl.multiple_of(place[0] * WINDOW, WINDOW), WINDOW)
    others = pl.ds(pl.multiple_of((1 - place[0]) * WINDOW, WINDOW), WINDOW)
    moves = [(k, packed.at[:count, :]), (v, packed.at[count : 2 * count, :])]
    for j in range(q.shape[1] // width):
        to = base + j * WINDOW
        moves.append((q.at[others, j * width : (j + 1) * width], packed.at[to : to + WINDOW, :]))
    copies = [pltpu.make_async_copy(source, target, sems.at[i]) for i, (source, target) in enumerate(moves)]
    for copy in copies:
        copy.start()
    shape = (BF16_ROWS, width)
    lane, row = (lax.broadcasted_iota(jnp.int32, shape, i) for i in (1, 0))
    left = jnp.zeros(shape, F32)
    for h in range(sink.shape[0]):
        left = jnp.where(lane == h, sink[h], left)
    terms = jnp.zeros(shape, F32)
    for i in range(3):
        term = left.astype(BF16).astype(F32)
        terms = jnp.where(row == i, term, terms)
        left = left - term
    packed[2 * count : base, :] = terms.astype(BF16)
    if code_rows:
        gains, table_ref = extra
        gains[...] = jnp.broadcast_to(gain[...], (WINDOW, gain.shape[1])).T
        expert = lax.broadcasted_iota(jnp.int32, (code_rows, WINDOW), 0)
        table = jnp.zeros((code_rows, WINDOW), F32)
        for i in range(TOP):
            named = jnp.broadcast_to(routes[i : i + 1, rows], expert.shape) == expert
            table += jnp.where(named, jnp.broadcast_to(codes[i : i + 1, rows], expert.shape).astype(F32), 0.0)
        table_ref[...] = table.astype(BF16)
    for copy in copies:
        copy.wait()


def pack(code_rows, place, sink_logit, norm_gain, routes, gate_codes, key_rows, values, queries):
    rows, width = key_rows.shape
    tall = queries.shape[1] // width * WINDOW
    shapes = [jax.ShapeDtypeStruct((2 * rows + BF16_ROWS + tall, width), BF16)]
    if code_rows:
        features = norm_gain.shape[0]
        shapes += [jax.ShapeDtypeStruct((features, WINDOW), F32), jax.ShapeDtypeStruct((code_rows, WINDOW), BF16)]
    return pl.pallas_call(
        functools.partial(pack_kernel, code_rows),
        out_shape=shapes,
        in_specs=[SMEM] * 2 + [VMEM] * 3 + [ANY] * 3,
        out_specs=[VMEM] * len(shapes),
        scratch_shapes=[pltpu.SemaphoreType.DMA((2 + tall // WINDOW,))],
        cost_estimate=pl.CostEstimate(flops=1, bytes_accessed=1, transcendentals=0),
        compiler_params=pltpu.CompilerParams(vmem_limit_bytes=16 * 2**20),
        name="pack",
    )(
        place, in_hbm(sink_logit), norm_gain[None, :], in_hbm(routes.T), in_hbm(gate_codes.T),
        in_hbm(key_rows), in_hbm(values), in_hbm(queries),
    )


def rim_kernel(k, v, rim, sems):
    last = k.shape[0] - WINDOW
    copies = [
        pltpu.make_async_copy(k.at[last:, :], rim.at[:WINDOW, :], sems.at[0]),
        pltpu.make_async_copy(v.at[last:, :], rim.at[WINDOW:, :], sems.at[1]),
    ]
    for copy in copies:
        copy.start()
    for copy in copies:
        copy.wait()


def pack_rim(key_rows, values):
    return pl.pallas_call(
        rim_kernel,
        out_shape=jax.ShapeDtypeStruct((2 * WINDOW, key_rows.shape[1]), BF16),
        in_specs=[ANY, ANY],
        out_specs=VMEM,
        scratch_shapes=[pltpu.SemaphoreType.DMA((2,))],
        cost_estimate=pl.CostEstimate(flops=0, bytes_accessed=4 * key_rows.size, transcendentals=0),
        compiler_params=pltpu.CompilerParams(vmem_limit_bytes=4 * 2**20),
        name="rim",
    )(in_hbm(key_rows), in_hbm(values))


def attend(place, packed, rim, q_blocks):
    core, first = place[0], place[1] == 1
    start = pl.multiple_of(core * WINDOW, WINDOW)
    lead = core == 0
    tall = q_blocks.shape[0]
    base = packed.shape[0] - tall
    count = (base - BF16_ROWS) // 2
    past = jnp.concatenate(
        [
            jnp.where(lead, rim[:WINDOW, :], packed[:WINDOW, :]),
            jnp.where(lead, rim[WINDOW:, :], packed[count : count + WINDOW, :]),
        ],
        axis=1,
    )
    later = pl.ds(pl.multiple_of(count + start, WINDOW), WINDOW)
    present = jnp.concatenate([packed[pl.ds(start, WINDOW), :], packed[later, :]], axis=1)
    terms = packed[2 * count : base, :].astype(F32)
    sinks = terms[0:1] + terms[1:2] + terms[2:3]
    q_cols = [(q_blocks[j : j + WINDOW] * HEAD_DIM ** (-0.5)).T for j in range(0, tall, WINDOW)]
    return heads_of(jnp.concatenate(q_cols, axis=0), past, present, sinks, first)


def front_own_kernel(place, packed, rim, q, ow, resid, out, q_held, ow_held, resid_held, sems):
    rows = pl.ds(pl.multiple_of(place[0] * WINDOW, WINDOW), WINDOW)
    width = packed.shape[1]
    moves = [
        (q.at[rows, j * width : (j + 1) * width], q_held.at[j * WINDOW : (j + 1) * WINDOW, :])
        for j in range(q.shape[1] // width)
    ]
    moves += [(ow, ow_held), (resid.at[:, rows], resid_held)]
    copies = [pltpu.make_async_copy(source, target, sems.at[i]) for i, (source, target) in enumerate(moves)]
    for copy in copies:
        copy.start()
    for copy in copies[:-2]:
        copy.wait()
    heads = attend(place, packed, rim, q_held[...])
    for copy in copies[-2:]:
        copy.wait()
    projected = jnp.dot(ow_held[...], heads, preferred_element_type=F32)
    out[...] = projected + resid_held[...].astype(F32)


def front_kernel(code_rows, place, packed, rim, ow, stream, *refs):
    base = packed.shape[0] - ow.shape[1] // packed.shape[1] * WINDOW
    heads = attend(place, packed, rim, packed[base:, :])
    attended = (stream[...] + jnp.dot(ow[...], heads, preferred_element_type=F32)).astype(BF16)
    if not code_rows:
        refs[0][...] = attended
        return
    gains, table, attended_ref, upper, lower = refs
    attended_ref[...] = attended
    widened = attended.astype(F32)
    spread = jnp.mean(widened * widened, axis=0, keepdims=True)
    normed = (widened * lax.rsqrt(spread + 1e-05) * gains[...]).astype(BF16)
    body = normed.shape[0] // WINDOW * WINDOW
    blocks = [normed[j : j + WINDOW].T for j in range(0, body, WINDOW)]
    parcel = jnp.concatenate([table[...], normed[body:], *blocks], axis=0)
    upper[...] = parcel[: upper.shape[0]]
    lower[...] = parcel[upper.shape[0] :]


def front(code_rows, queries, key_rows, values, sink_logit, o_weight, residual, norm_gain, routes, gate_codes, weights):
    seq, core = lax.axis_index("seq"), lax.axis_index("exp")
    place = jnp.stack([core, jnp.where((seq == 0) & (core == 0), 1, 0)]).astype(jnp.int32)
    ow_b = swapped(o_weight.T)
    steps = [(s, s + 1) for s in range(lax.axis_size("seq") - 1)]
    rim_a = lax.ppermute(pack_rim(key_rows, values), "seq", steps)
    packed, *extra = pack(
        code_rows, place, sink_logit, norm_gain, routes, gate_codes, key_rows, values, queries
    )
    weights, packed = after(weights, packed)
    packed, rim_a = after(packed, rim_a)
    packed_b, rim_b = swapped(packed), swapped(rim_a)
    features = residual.shape[1]
    half = half_of(features)
    blocks = queries.shape[1] // packed.shape[1]
    held = ((blocks * WINDOW, packed.shape[1]), o_weight.T.shape, (features, WINDOW))
    cost = pl.CostEstimate(flops=1, bytes_accessed=1, transcendentals=0)
    params = pltpu.CompilerParams(vmem_limit_bytes=20 * 2**20)
    stream = pl.pallas_call(
        front_own_kernel,
        out_shape=jax.ShapeDtypeStruct((features, WINDOW), F32),
        in_specs=[SMEM] + [VMEM] * 2 + [ANY] * 3,
        out_specs=VMEM,
        scratch_shapes=[pltpu.VMEM(shape, BF16) for shape in held] + [pltpu.SemaphoreType.DMA((blocks + 2,))],
        cost_estimate=cost,
        compiler_params=params,
        name="front_own",
    )(place, packed, rim_a, in_hbm(queries), in_hbm(o_weight.T), in_hbm(residual.T))
    shapes = [(features, WINDOW)]
    if code_rows:
        shapes += [(code_rows + half, WINDOW), (features - half, WINDOW)]
    outs = pl.pallas_call(
        functools.partial(front_kernel, code_rows),
        out_shape=[jax.ShapeDtypeStruct(shape, BF16) for shape in shapes],
        in_specs=[SMEM] + [VMEM] * (4 + len(extra)),
        out_specs=[VMEM] * len(shapes),
        cost_estimate=cost,
        compiler_params=params,
        name="front",
    )(place, packed_b, rim_b, in_vmem(ow_b), stream, *extra)
    return outs, weights


def swapped(value):
    return lax.ppermute(value, "exp", [(0, 1), (1, 0)])


def after(value, earlier):
    return lax.optimization_barrier((value, earlier))


def rms_norm(stream, norm_gain):
    widened = stream.astype(F32)
    spread = jnp.mean(widened * widened, axis=-1, keepdims=True)
    return (widened * lax.rsqrt(spread + 1e-05) * norm_gain).astype(BF16)


def expert_kernel(code_rows, place, upper, lower, *refs):
    weights, (out_upper, out_lower) = refs[:6], refs[6:]
    parcel = jnp.concatenate([upper[...], lower[...]], axis=0)
    body = (parcel.shape[0] - code_rows) // WINDOW * WINDOW
    head = parcel.shape[0] - body
    blocks = [parcel[j : j + WINDOW] for j in range(head, head + body, WINDOW)]
    over = parcel[:head].T
    rows = jnp.concatenate([*blocks, over[:, code_rows:]], axis=1)
    total = None
    for w_gate, w_up, w_down in (weights[:3], weights[3:]):
        gate_val = jnp.dot(rows, w_gate[...], preferred_element_type=F32)
        up_val = jnp.dot(rows, w_up[...], preferred_element_type=F32)
        hidden = swiglu(gate_val, up_val).astype(BF16)
        term = jnp.dot(hidden, w_down[...], preferred_element_type=F32)
        total = term if total is None else total + term
    codes = over[:, :code_rows].astype(F32)
    mine = lax.broadcasted_iota(jnp.int32, codes.shape, 1) == place[0]
    code = jnp.sum(jnp.where(mine, codes, 0.0), axis=1, keepdims=True)
    terms = (total * (code / jnp.sum(codes, axis=1, keepdims=True))).astype(BF16)
    blocks = [terms[:, j : j + WINDOW] for j in range(0, body, WINDOW)]
    terms = jnp.concatenate([terms[:, body:].T, *blocks], axis=0)
    half = out_upper.shape[0]
    out_upper[...] = terms[:half]
    out_lower[...] = terms[half:]


def expert_terms(code_rows, expert, weights, parcel):
    half, rest = parcel[0].shape[0] - code_rows, parcel[1].shape[0]
    return pl.pallas_call(
        functools.partial(expert_kernel, code_rows),
        out_shape=[jax.ShapeDtypeStruct((n, WINDOW), BF16) for n in (half, rest)],
        in_specs=[SMEM] + [VMEM] * 8,
        out_specs=[VMEM] * 2,
        cost_estimate=pl.CostEstimate(flops=10**9, bytes_accessed=1, transcendentals=0),
        compiler_params=pltpu.CompilerParams(vmem_limit_bytes=24 * 2**20),
        name="experts",
    )(expert, *parcel, *weights)


def total_kernel(*refs):
    uppers, lowers, out = refs[:3], refs[3:6], refs[6]
    summed = [sum(ref[...].astype(F32) for ref in half) for half in (uppers, lowers)]
    summed = jnp.concatenate(summed, axis=0).astype(BF16)
    head = summed.shape[0] % WINDOW
    body = summed.shape[0] - head
    for j in range(0, body, WINDOW):
        out[j : j + WINDOW, :] = summed[head + j : head + j + WINDOW].T
    if head:
        out[body:, :] = summed[:head]


def total_of(uppers, lowers):
    features = uppers[0].shape[0] + lowers[0].shape[0]
    return pl.pallas_call(
        total_kernel,
        out_shape=jax.ShapeDtypeStruct((features, WINDOW), BF16),
        in_specs=[VMEM] * 6,
        out_specs=VMEM,
        cost_estimate=pl.CostEstimate(flops=1, bytes_accessed=1, transcendentals=0),
        compiler_params=pltpu.CompilerParams(vmem_limit_bytes=16 * 2**20),
        name="total",
    )(*uppers, *lowers)


def half_of(features):
    return features // 2 // BF16_ROWS * BF16_ROWS


def ring_of(count, cores):
    order = list(range(0, count, 2)) + list(range(count - 1, 0, -2))
    right = [(order[i], order[(i + 1) % count], core) for i in range(count) for core in range(cores)]
    steps = [(s * cores + c, t * cores + c) if c % 2 == 0 else (t * cores + c, s * cores + c) for s, t, c in right]
    return steps, [(target, source) for source, target in steps]


def add(a, b):
    return (a.astype(F32) + b.astype(F32)).astype(BF16)


def mixed_by_ring(parcel, code_rows, weights):
    count = lax.axis_size("seq")
    right, left = ring_of(count, lax.axis_size("exp"))
    far = count // 2
    expert = lax.axis_index("seq").astype(jnp.int32)[None]
    to_right = functools.partial(lax.ppermute, axis_name=("seq", "exp"), perm=right)
    to_left = functools.partial(lax.ppermute, axis_name=("seq", "exp"), perm=left)
    apply = functools.partial(expert_terms, code_rows, expert, weights)
    at = {0: parcel}
    at[-1], at[1] = [to_right(half) for half in parcel], [to_left(half) for half in parcel]
    terms = {}

    def work(k, arrived):
        at[k], arrived = after(at[k], arrived)
        terms[k] = apply(at[k])
        return arrived

    last = 0
    terms[0] = apply(parcel)
    for k in range(2, far + 1):
        uppers, lowers = (at[1 - k][0], at[k - 1][0]), (at[1 - k][1], at[k - 1][1])
        uppers, terms[last] = after(uppers, terms[last])
        upper_left = to_right(uppers[0])
        upper_right = to_left(uppers[1]) if k < far else None
        if 2 < k == far:
            uppers = work(k - 2, uppers)
            lowers, terms[k - 2] = after(lowers, terms[k - 2])
        lower_left = to_right(lowers[0]) if k < far else None
        lower_right = to_left(lowers[1])
        at[1 - k], at[k - 1] = (uppers[0], lowers[0]), (uppers[1], lowers[1])
        if k < far:
            last = 1 - k
            terms[last] = apply(at[last])
        at[-k], at[k] = (upper_left, lower_left), (upper_right, lower_right)
    opposite = (at[-far][0], at[far][1])
    terms[far - 1] = apply(at[far - 1])
    right_low = to_right(terms[far - 1][1])
    terms[far - 1] = work(1 - far, terms[far - 1])
    left_up = to_left(terms[1 - far][0])
    opposite, terms[1 - far] = after(opposite, terms[1 - far])
    farthest = apply(opposite)
    right_up, left_low = to_right(farthest[0]), to_left(farthest[1])
    for k in range(1, far - 2):
        farthest = work(k, farthest)
        (left_up, right_low), terms[k] = after((left_up, right_low), terms[k])
    for k in range(far - 1, 0, -1):
        right_up = to_right(add(terms[k][0], right_up))
        left_low = to_left(add(terms[-k][1], left_low))
        if k > 1:
            right_low = to_right(add(terms[k - 1][1], right_low))
            left_up = to_left(add(terms[1 - k][0], left_up))
    near, final = after((terms[0], left_up, right_low), (left_low, right_up))
    (upper, lower), left_up, right_low = near
    left_low, right_up = final
    return total_of((upper, left_up, right_up), (lower, left_low, right_low))


def pack_rows(normed, expert_ids, gate_codes, expert_count, capacity):
    pair_ids = expert_ids.reshape(-1)
    matches = (pair_ids[:, None] == jnp.arange(expert_count, dtype=jnp.int32)[None, :]).astype(
        jnp.int32
    )
    within = jnp.sum((jnp.cumsum(matches, axis=0) - 1) * matches, axis=1)
    sources = normed[jnp.arange(pair_ids.shape[0], dtype=jnp.int32) // expert_ids.shape[1]]
    outbox = jnp.zeros((expert_count * capacity, normed.shape[1]), normed.dtype)
    outbox = outbox.at[pair_ids * capacity + within].set(sources)
    code_vals = gate_codes.astype(F32)
    shares = (code_vals / jnp.sum(code_vals, axis=1, keepdims=True)).reshape(-1)
    return (outbox, pair_ids, within, shares)


def mixed_by_packing(normed, routes, gate_codes, weights, expert_count, capacity):
    w_gate, w_up, w_down = weights
    owners, block = lax.axis_size("exp"), normed.shape[0]
    owner_pos = lax.axis_index("exp")
    own = lambda value: lax.dynamic_slice_in_dim(value, owner_pos * block, block, 0)
    outbox, pair_ids, within, shares = pack_rows(
        normed, own(routes), own(gate_codes), expert_count, capacity
    )
    outbox = outbox.reshape(expert_count, capacity, normed.shape[1])
    exchange = functools.partial(lax.all_to_all, axis_name="seq", split_axis=0, concat_axis=0, tiled=True)
    arrived = lax.all_gather(exchange(outbox), "exp", axis=0, tiled=True)
    flat_rows = arrived.reshape(-1, arrived.shape[-1])
    gate_val = jnp.dot(flat_rows, w_gate, preferred_element_type=F32)
    up_val = jnp.dot(flat_rows, w_up, preferred_element_type=F32)
    hidden = swiglu(gate_val, up_val).astype(BF16)
    partial_value = jnp.dot(hidden, w_down, preferred_element_type=F32).reshape(arrived.shape)
    whole = lax.psum_scatter(partial_value.astype(BF16), "exp", scatter_dimension=0, tiled=True)
    picked = exchange(whole)[pair_ids, within].astype(F32)
    mixture = jnp.sum((picked * shares[:, None]).reshape(-1, TOP, normed.shape[1]), axis=1)
    return mixture.astype(BF16)


def local(
    queries,
    key_rows,
    values,
    sink_logit,
    o_weight,
    residual,
    norm_gain,
    routes,
    gate_codes,
    w_gate,
    w_up,
    w_down,
):
    block_rows = residual.shape[0] // lax.axis_size("exp")
    expert_count = w_gate.shape[0] * lax.axis_size("seq")
    capacity = max(2, 2 * block_rows * TOP // expert_count)
    weights = (w_gate[0], w_up[0], w_down[0])
    attention = (queries, key_rows, values, sink_logit, o_weight, residual, norm_gain, routes, gate_codes)
    if capacity < block_rows:
        (attended,), weights = front(0, *attention, weights)
        attended = attended.T
        normed = rms_norm(attended, norm_gain)
        return (attended, mixed_by_packing(normed, routes, gate_codes, weights, expert_count, capacity))
    code_rows = -(-expert_count // BF16_ROWS) * BF16_ROWS
    (attended, *parcel), weights = front(code_rows, *attention, weights)
    gate_b, up_b = swapped(weights[0]), swapped(weights[1])
    down, parcel = after(weights[2], parcel)
    down_b = swapped(down)
    weights = [in_vmem(weight) for weight in (*weights, gate_b, up_b, down_b)]
    return (attended.T, mixed_by_ring(parcel, code_rows, weights).T)


def solution(mesh):
    placed = (
        P(("groups", "seq"), "exp"),
        P(("groups", "seq"), "exp"),
        P(("groups", "seq"), "exp"),
        P("exp"),
        P("exp", None),
        P(("groups", "seq"), None),
        P(),
        P(("groups", "seq"), None),
        P(("groups", "seq"), None),
        P("seq", None, "exp"),
        P("seq", None, "exp"),
        P("seq", "exp", None),
    )
    return jax.shard_map(
        local,
        mesh=mesh,
        in_specs=placed,
        out_specs=(P(("groups", "seq", "exp"), None), P(("groups", "seq", "exp"), None)),
        check_vma=False,
    )
```
